32 devices in a mesh: seqin: 4 (over y, x), seqout: 2 (over core), head: 4 (over z).
Axes of the slice: x: 2, y: 2, z: 4, core: 2. Of those that a mesh axis runs over, the one named last changes fastest.
Arguments:
- queries: bfloat16 [8192, 4096], P(('seqin', 'seqout'), 'head'), may hold values from -6 to 6
- keys: bfloat16 [8192, 4096], P(('seqin', 'seqout'), 'head'), may hold values from -6 to 6
- values: bfloat16 [8192, 4096], P(('seqin', 'seqout'), 'head'), may hold values from -120 to 120
- gain: float32 [4096], P('head'), may hold values from 0.5 to 1.5
- cotangent: bfloat16 [8192, 4096], P(('seqin', 'seqout'), 'head'), may hold values from -6 to 6
Outputs:
- mixed: bfloat16 [8192, 4096], P(('seqin', 'seqout'), 'head')
- grad_queries: bfloat16 [8192, 4096], P(('seqin', 'seqout'), 'head')
- grad_keys: bfloat16 [8192, 4096], P(('seqin', 'seqout'), 'head')
- grad_values: bfloat16 [8192, 4096], P(('seqin', 'seqout'), 'head')
The draws below stay inside these ranges and needn't reach their ends.
All inputs are finite; a program needn't handle non-finite values.
Results may differ from the reference program's by a relative error of at most 0.0089.
Values sent between devices are 32-bit elements; how exact they have to be, the bound alone decides.
A program may use at most 192 MiB of HBM per device.

```python
import math
import jax
import jax.numpy as jnp
from jax import lax

H = 32
E = 128
D = 4096
BLOCK = 512
TOKENS = 8192


def draw_values(key, part):
    key = jax.random.fold_in(key, 7)
    first, second, third = jax.random.split(key, 3)
    base = jnp.clip(jax.random.normal(first, (TOKENS, D), jnp.float32), -4.0, 4.0)
    rise = math.log(3.0)
    rows = jnp.exp(jax.random.uniform(second, (TOKENS, 1), jnp.float32) * math.log(10.0))
    ramp = jnp.arange(D, dtype=jnp.float32)[None, :] / (D - 1)
    cols = jnp.exp(rise * ramp) * jnp.exp(jax.random.uniform(third, (1, D), jnp.float32) * math.log(4.0))
    return (base * rows * cols / 6.0).astype(jnp.bfloat16)


def levels(own_key, dims, pieces, smallest, high):
    level, own = 1.0, jax.random.fold_in(own_key, 6)
    for axis_at, shards_of in pieces:
        heights = jnp.exp(jax.random.uniform(jax.random.fold_in(own, axis_at), (shards_of,), jnp.float32, smallest / len(pieces), high / len(pieces)))
        level = level * jnp.repeat(heights, dims[axis_at] // shards_of).reshape([-1 if axis == axis_at else 1 for axis in range(len(dims))])
    return level


def noise(stream_key, shape, scale, limit, cuts=(), held_as=jnp.bfloat16):
    drawn = scale * jax.random.normal(stream_key, shape, jnp.float32)
    if cuts:
        drawn = drawn * levels(stream_key, shape, cuts, -0.22, 0.18)
    return jnp.clip(drawn, -limit, limit).astype(held_as)


def setup_inputs(seed: int = 0) -> dict:
    streams_of = jax.random.split(jax.random.key(seed), 6)
    return {
        "queries": noise(streams_of[0], (TOKENS, D), 1.0, 6.0, ((0, 8), (1, 4))),
        "keys": noise(streams_of[1], (TOKENS, D), 1.0, 6.0, ((0, 8), (1, 4))),
        "values": draw_values(jax.random.fold_in(streams_of[5], 71), 0),
        "gain": jnp.clip(1.0 + 0.1 * jax.random.normal(streams_of[3], (D,), jnp.float32), 0.5, 1.5),
        "cotangent": noise(streams_of[4], (TOKENS, D), 1.0, 6.0, ((0, 8), (1, 4))),
    }


HIGH = lax.Precision.HIGHEST

def features(x):
    xf = x.astype(jnp.float32)
    return jnp.where(xf > 0, xf + 1.0, jnp.exp(jnp.minimum(xf, 0.0))).astype(jnp.bfloat16)

def slope(x):
    xf = x.astype(jnp.float32)
    return jnp.where(xf > 0, 1.0, jnp.exp(jnp.minimum(xf, 0.0)))

def reference(queries, keys, values, gain, cotangent):
    nblk = TOKENS // BLOCK
    shape4 = (nblk, BLOCK, H, E)
    fq = features(queries).reshape(shape4)
    fk = features(keys).reshape(shape4)
    vv = values.reshape(shape4)
    causal = jnp.arange(BLOCK)[:, None] >= jnp.arange(BLOCK)[None, :]

    def forward(carry, blk):
        state, norm = carry
        bq, bk, bv = blk
        bq32 = bq.astype(jnp.float32)
        bk32 = bk.astype(jnp.float32)
        bv32 = bv.astype(jnp.float32)
        scores = jnp.einsum('thd,shd->hts', bq32, bk32)
        wts = jnp.where(causal[None], scores, 0.0).astype(jnp.bfloat16).astype(jnp.float32)
        numer = jnp.einsum('hts,she->the', wts, bv32) + jnp.einsum('thd,hde->the', bq32, state, precision=HIGH)
        denom = jnp.einsum('hts->th', wts) + jnp.einsum('thd,hd->th', bq32, norm, precision=HIGH)
        attn = numer / denom[:, :, None]
        new_state = state + jnp.einsum('shd,she->hde', bk32, bv32)
        new_norm = norm + lax.optimization_barrier(jnp.sum(bk32, axis=0))
        return ((new_state, new_norm), (attn, denom, state, norm))
    init = (jnp.zeros((H, E, E), jnp.float32), jnp.zeros((H, E), jnp.float32))
    _, (attn, denom, states, norms) = lax.scan(forward, init, (fq, fk, vv))
    flat = attn.reshape(TOKENS, D)
    scale = lax.rsqrt(lax.optimization_barrier(jnp.sum(flat * flat, axis=1)) / D + 1e-06)
    mixed = (flat * scale[:, None] * gain[None, :]).astype(jnp.bfloat16)
    weighted = cotangent.astype(jnp.float32) * gain[None, :]
    proj = lax.optimization_barrier(jnp.sum(weighted * flat, axis=1))
    d_attn = scale[:, None] * weighted - flat * (scale ** 3 * proj / D)[:, None]
    d4 = d_attn.reshape(nblk, BLOCK, H, E)
    g_num = (d4 / denom[..., None]).astype(jnp.bfloat16)
    g_den = -lax.optimization_barrier(jnp.sum(d4 * attn, axis=3)) / denom

    def backward(carry, blk):
        later, later_den = carry
        bq, bk, bv, gn, gd, state, norm = blk
        bq32 = bq.astype(jnp.float32)
        bk32 = bk.astype(jnp.float32)
        bv32 = bv.astype(jnp.float32)
        gn32 = gn.astype(jnp.float32)
        scores = jnp.einsum('thd,shd->hts', bq32, bk32)
        wts = jnp.where(causal[None], scores, 0.0).astype(jnp.bfloat16).astype(jnp.float32)
        mix = jnp.einsum('the,she->hts', gn32, bv32) + gd.T[:, :, None]
        mixw = jnp.where(causal[None], mix, 0.0).astype(jnp.bfloat16).astype(jnp.float32)
        dfq = jnp.einsum('hts,shd->thd', mixw, bk32) + jnp.einsum('the,hde->thd', gn32, state, precision=HIGH) + gd[:, :, None] * norm[None]
        dfk = jnp.einsum('hts,thd->shd', mixw, bq32) + jnp.einsum('hde,she->shd', later, bv32, precision=HIGH) + later_den[None]
        dvv = jnp.einsum('hts,the->she', wts, gn32) + jnp.einsum('shd,hde->she', bk32, later, precision=HIGH)
        new_later = later + jnp.einsum('thd,the->hde', bq32, gn32)
        new_den = later_den + jnp.einsum('th,thd->hd', gd, bq32, precision=HIGH)
        return ((new_later, new_den), (dfq, dfk, dvv))
    _, (dfq, dfk, dvv) = lax.scan(backward, init, (fq, fk, vv, g_num, g_den, states, norms), reverse=True)
    grad_queries = (dfq.reshape(TOKENS, D) * slope(queries)).astype(jnp.bfloat16)
    grad_keys = (dfk.reshape(TOKENS, D) * slope(keys)).astype(jnp.bfloat16)
    grad_values = dvv.reshape(TOKENS, D).astype(jnp.bfloat16)
    return (mixed, grad_queries, grad_keys, grad_values)
```

```python
import functools

import jax
import jax.numpy as jnp
from jax import lax
from jax.experimental import pallas as pl
from jax.experimental.pallas import tpu as pltpu
from jax.sharding import PartitionSpec as P

E = 128
BLOCK = 512
NORM = E
PAY = E + 8
F32 = jnp.float32
BF16 = jnp.bfloat16
MESH = pl.DeviceIdType.MESH


def features(x):
    xf = x.astype(F32)
    return jnp.where(xf > 0, xf + 1.0, jnp.exp(jnp.minimum(xf, 0.0))).astype(BF16)


def slope(x):
    return jnp.exp(jnp.minimum(x.astype(F32), 0.0))


def dot(a, b, ca=1, cb=0):
    return lax.dot_general(a, b, (((ca,), (cb,)), ((), ())), preferred_element_type=F32)


def split(x):
    hi = x.astype(BF16)
    return hi, (x - hi.astype(F32)).astype(BF16)


def kernel(dims, q_hbm, k_hbm, v_hbm, gain_ref, c_hbm, mixed_hbm, gq_hbm, gk_hbm, gv_hbm,
           qv, kv, vv, cv, fq, fk, wts, att, den, gn, dvp, om, oq, ok, ov,
           kvb, rvb, sh, tot, r0, tx, rx, fin, pfx, stat, stat_in, scl,
           in_sem, out_sem, s0, q0, sx, rxs, s2, q2, ss, rs):
    heads, nblk, block, n_in, n_out, n_head, width = dims
    half = heads // 2
    tile = block // 2
    n_seq = n_in * n_out
    nchips = n_seq // 2
    stages = nchips.bit_length() - 1
    a_in, a_out, a_head = lax.axis_index("seqin"), lax.axis_index("seqout"), lax.axis_index("head")
    me = a_in * n_out + a_out
    core = lax.rem(me, 2)
    mine = core * half
    theirs = (1 - core) * half

    def bit(m):
        return lax.rem(lax.div(me, m), 2)

    def peer(m):
        other = me + m - 2 * m * bit(m)
        return (lax.div(other, n_out), lax.rem(other, n_out), a_head)

    def zpeer(d):
        return (a_in, a_out, lax.rem(a_head + d, n_head))

    def fetch(array, h):
        src, dst = ((k_hbm, kv), (v_hbm, vv), (q_hbm, qv), (c_hbm, cv))[array]
        cols = pl.ds(pl.multiple_of(h * E, E), E)
        return pltpu.make_async_copy(src.at[:, cols], dst.at[h], in_sem.at[array, h])

    def put(array, h):
        src, dst = ((om, mixed_hbm), (oq, gq_hbm), (ok, gk_hbm), (ov, gv_hbm))[array]
        cols = pl.ds(pl.multiple_of(h * E, E), E)
        return pltpu.make_async_copy(src.at[h], dst.at[:, cols], out_sem.at[array, h])

    def each(n, body):
        def step(j, carry):
            body(j)
            return carry
        lax.fori_loop(0, n, step, 0)

    def order(j):
        return lax.rem(theirs + j, heads)

    def start_kv(j):
        fetch(0, order(j)).start()
        fetch(1, order(j)).start()

    def start_qc(h):
        fetch(2, h).start()
        fetch(3, h).start()

    each(heads, start_kv)
    each(heads, start_qc)

    barrier = pltpu.get_barrier_semaphore()
    masks = [1 << s for s in range(stages + 1)]
    for m in masks:
        pl.semaphore_signal(barrier, inc=1, device_id=peer(m), device_id_type=MESH)
    for d in range(1, n_head):
        pl.semaphore_signal(barrier, inc=1, device_id=zpeer(d), device_id_type=MESH)

    def swap(dirn, j):
        return pltpu.make_async_remote_copy(
            src_ref=tot.at[dirn, theirs + j], dst_ref=r0.at[dirn, j],
            send_sem=s0.at[dirn, j], recv_sem=q0.at[dirn, j],
            device_id=peer(1), device_id_type=MESH)

    def hop(dirn, s, j):
        return pltpu.make_async_remote_copy(
            src_ref=tx.at[dirn, s, j], dst_ref=rx.at[dirn, s, j],
            send_sem=sx.at[dirn, s, j], recv_sem=rxs.at[dirn, s, j],
            device_id=peer(2 << s), device_id_type=MESH)

    def back(dirn, j):
        return pltpu.make_async_remote_copy(
            src_ref=fin.at[dirn, j], dst_ref=pfx.at[dirn, mine + j],
            send_sem=s2.at[dirn, j], recv_sem=q2.at[dirn, j],
            device_id=peer(1), device_id_type=MESH)

    def back_in(dirn, j):
        return pltpu.make_async_remote_copy(
            src_ref=fin.at[dirn, j], dst_ref=pfx.at[dirn, theirs + j],
            send_sem=s2.at[dirn, j], recv_sem=q2.at[dirn, j],
            device_id=peer(1), device_id_type=MESH)

    def chip_total(dirn):
        def body(j):
            swap(dirn, j).wait_recv()
            tx[dirn, 0, j] = tot[dirn, mine + j] + r0[dirn, j]
            hop(dirn, 0, j).start()
        each(half, body)

    def hop_on(dirn, s):
        def body(j):
            hop(dirn, s, j).wait_recv()
            if s + 1 < stages:
                tx[dirn, s + 1, j] = tx[dirn, s, j] + rx[dirn, s, j]
                hop(dirn, s + 1, j).start()
                return
            total = jnp.zeros((PAY, E), F32)
            for i in range(stages):
                before = bit(2 << i) == 1 - dirn
                total = total + jnp.where(before, rx[dirn, i, j], 0.0)
            near = core == dirn
            own, other = tot[dirn, mine + j], r0[dirn, j]
            fin[dirn, j] = total + jnp.where(near, own, 0.0)
            pfx[dirn, mine + j] = total + jnp.where(near, 0.0, other)
            back(dirn, j).start()
        each(half, body)

    def arrive(dirn):
        each(half, lambda j: back_in(dirn, j).wait_recv())

    def drain(dirn):
        def body(j):
            swap(dirn, j).wait_send()
            for s in range(stages):
                hop(dirn, s, j).wait_send()
            back(dirn, j).wait_send()
        each(half, body)

    def rows(b):
        return pl.ds(b * block, block)

    def key_sums(h):
        fetch(0, h).wait()
        fetch(1, h).wait()
        total = jnp.zeros((PAY, E), F32)
        for b in range(nblk):
            f = features(kv[h, rows(b), :])
            fk[h, rows(b), :] = f
            state = dot(f, vv[h, rows(b), :], 0, 0)
            norm = jnp.sum(f.astype(F32), axis=0, keepdims=True)
            part = jnp.concatenate([state, jnp.broadcast_to(norm, (8, E))], axis=0)
            kvb[h, b] = part
            total = total + part
        tot[0, h] = total

    def causal():
        return (lax.broadcasted_iota(jnp.int32, (tile, tile), 0)
                >= lax.broadcasted_iota(jnp.int32, (tile, tile), 1))

    def forward_local(h):
        fetch(2, h).wait()
        keep = causal()
        ones = jnp.ones((block, E), BF16)
        for b in range(nblk):
            base = b * block
            f = features(qv[h, rows(b), :])
            fq[h, rows(b), :] = f
            g = fk[h, rows(b), :]
            va = jnp.concatenate([vv[h, rows(b), :], ones], axis=1)
            top = jnp.where(keep, dot(f[:tile], g[:tile], 1, 1), 0.0).astype(BF16)
            low = dot(f[tile:], g, 1, 1)
            left = low[:, :tile].astype(BF16)
            right = jnp.where(keep, low[:, tile:], 0.0).astype(BF16)
            wts[h, b, 0] = top
            wts[h, b, 1] = left
            wts[h, b, 2] = right
            up = dot(top, va[:tile])
            down = dot(jnp.concatenate([left, right], axis=1), va)
            att[h, pl.ds(base, tile), :] = up[:, :E]
            den[h, pl.ds(base, tile), :] = up[:, E:]
            att[h, pl.ds(base + tile, tile), :] = down[:, :E]
            den[h, pl.ds(base + tile, tile), :] = down[:, E:]

    def forward_state(b):
        def body(h, sums):
            sq, pr = sums
            if b == 0:
                fetch(3, h).wait()
            full = pfx[0, h]
            for a in range(b):
                full = full + kvb[h, a]
            hi, lo = split(full[:E])
            sh[h, b] = jnp.concatenate([hi, lo], axis=1)
            norm = jnp.transpose(jnp.broadcast_to(full[NORM:NORM + 1], (E, E)))
            nhi, nlo = split(norm)
            wide = jnp.concatenate([jnp.concatenate([hi, nhi], axis=1),
                                    jnp.concatenate([lo, nlo], axis=1)], axis=0)
            f = fq[h, rows(b), :]
            both = dot(jnp.concatenate([f, f], axis=1), wide)
            inv = 1.0 / (den[h, rows(b), :] + both[:, E:])
            out = (att[h, rows(b), :] + both[:, :E]) * inv
            den[h, rows(b), :] = inv
            att[h, rows(b), :] = out
            w = cv[h, rows(b), :].astype(F32) * gain_ref[pl.ds(h, 1), :]
            return sq + out * out, pr + w * out
        zero = jnp.zeros((block, E), F32)
        sq, pr = lax.fori_loop(0, heads, body, (zero, zero))
        stat[b, 0:1, :] = jnp.sum(jnp.transpose(sq), axis=0, keepdims=True)
        stat[b, 1:2, :] = jnp.sum(jnp.transpose(pr), axis=0, keepdims=True)

    def share(b, d):
        return pltpu.make_async_remote_copy(
            src_ref=stat.at[b], dst_ref=stat_in.at[b, d - 1],
            send_sem=ss.at[b, d - 1], recv_sem=rs.at[b, d - 1],
            device_id=zpeer(d), device_id_type=MESH)

    def scales(b):
        for d in range(1, n_head):
            share(b, d).wait_recv()
        total = stat[b]
        for d in range(1, n_head):
            total = total + stat_in[b, d - 1]
        scale = lax.rsqrt(total[0:1] / width + 1e-06)
        pull = scale * scale * scale * total[1:2] / width
        scl[b, 0] = jnp.transpose(jnp.broadcast_to(scale, (E, block)))
        scl[b, 1] = jnp.transpose(jnp.broadcast_to(pull, (E, block)))

    def gradient(h):
        total = jnp.zeros((PAY, E), F32)
        gain = gain_ref[pl.ds(h, 1), :]
        for b in range(nblk):
            scale, pull = scl[b, 0], scl[b, 1]
            out, inv = att[h, rows(b), :], den[h, rows(b), :]
            sg = scale * gain
            om[h, rows(b), :] = (out * sg).astype(BF16)
            d = sg * cv[h, rows(b), :].astype(F32) - out * pull
            g = (d * inv).astype(BF16)
            gd = -jnp.sum(d * out, axis=1, keepdims=True) * inv
            gn[h, rows(b), :] = g
            den[h, rows(b), :] = gd
            f = fq[h, rows(b), :]
            later = dot(f, g, 0, 0)
            lden = jnp.sum(gd * f.astype(F32), axis=0, keepdims=True)
            part = jnp.concatenate([later, jnp.broadcast_to(lden, (8, E))], axis=0)
            rvb[h, b] = part
            total = total + part
        tot[1, h] = total
        put(0, h).start()

    def backward_local(h):
        keep = causal()
        for b in range(nblk):
            base = b * block
            f, k, v, g = fq[h, rows(b), :], fk[h, rows(b), :], vv[h, rows(b), :], gn[h, rows(b), :]
            gd = den[h, rows(b), :]
            gw = jnp.concatenate([gd] * (tile // E), axis=1)
            top = jnp.where(keep, dot(g[:tile], v[:tile], 1, 1) + gw[:tile], 0.0).astype(BF16)
            low = dot(g[tile:], v, 1, 1)
            left = (low[:, :tile] + gw[tile:]).astype(BF16)
            right = jnp.where(keep, low[:, tile:] + gw[tile:], 0.0).astype(BF16)
            norm = pfx[0, h, NORM:NORM + 1, :]
            for a in range(b):
                norm = norm + kvb[h, a, NORM:NORM + 1, :]
            far = dot(jnp.concatenate([g, g], axis=1), sh[h, b], 1, 1) + gd * norm
            up = dot(top, k[:tile]) + far[:tile]
            down = dot(jnp.concatenate([left, right], axis=1), k) + far[tile:]
            sl = slope(qv[h, rows(b), :])
            oq[h, pl.ds(base, tile), :] = (up * sl[:tile]).astype(BF16)
            oq[h, pl.ds(base + tile, tile), :] = (down * sl[tile:]).astype(BF16)
            att[h, pl.ds(base, tile), :] = dot(jnp.concatenate([top, left], axis=0), f, 0, 0)
            att[h, pl.ds(base + tile, tile), :] = dot(right, f[tile:], 0, 0)
            first = jnp.concatenate([wts[h, b, 0], wts[h, b, 1]], axis=0)
            dvp[h, pl.ds(base, tile), :] = dot(first, g, 0, 0)
            dvp[h, pl.ds(base + tile, tile), :] = dot(wts[h, b, 2], g[tile:], 0, 0)
        put(1, h).start()

    def backward_state(h):
        for b in range(nblk):
            full = pfx[1, h]
            for a in range(b + 1, nblk):
                full = full + rvb[h, a]
            hi, lo = split(full[:E])
            v, k = vv[h, rows(b), :], fk[h, rows(b), :]
            dk = dot(jnp.concatenate([v, v], axis=1), jnp.concatenate([hi, lo], axis=1), 1, 1)
            dk = dk + att[h, rows(b), :] + full[NORM:NORM + 1]
            ok[h, rows(b), :] = (dk * slope(kv[h, rows(b), :])).astype(BF16)
            dv = dot(jnp.concatenate([k, k], axis=1), jnp.concatenate([hi, lo], axis=0))
            ov[h, rows(b), :] = (dv + dvp[h, rows(b), :]).astype(BF16)
        put(2, h).start()
        put(3, h).start()

    def middle(dirn, local):
        chip_total(dirn)
        per = heads // (stages + 1)
        at = 0
        for s in range(stages):
            low, count = at, per
            at += per
            each(count, lambda j, low=low: local(low + j))
            hop_on(dirn, s)
        each(heads - at, lambda j: local(at + j))
        arrive(dirn)

    def theirs_first(dirn, body):
        def one(j):
            body(theirs + j)
            swap(dirn, j).start()
        each(half, one)
        each(half, lambda j: body(mine + j))

    greeted = len(masks) + n_head - 1

    def one_ready(j):
        key_sums(theirs + j)

    each(half, one_ready)
    pl.semaphore_wait(barrier, greeted)
    each(half, lambda j: swap(0, j).start())
    each(half, lambda j: key_sums(mine + j))
    middle(0, forward_local)
    for b in range(nblk):
        forward_state(b)
        for d in range(1, n_head):
            share(b, d).start()
    for b in range(nblk):
        scales(b)
    theirs_first(1, gradient)
    middle(1, backward_local)
    each(heads, backward_state)

    drain(0)
    drain(1)
    for b in range(nblk):
        for d in range(1, n_head):
            share(b, d).wait_send()

    def finish(h):
        for array in range(4):
            put(array, h).wait()
    each(heads, finish)


def shards(sizes, queries, keys, values, gain, cotangent):
    n_in, n_out, n_head = sizes
    rows, width = queries.shape
    heads = width // E
    block = min(BLOCK, rows)
    nblk = rows // block
    half = heads // 2
    stages = max((n_in * n_out // 2).bit_length() - 1, 1)
    dims = (heads, nblk, block, n_in, n_out, n_head, width * n_head)
    whole = (heads, rows, E)
    anywhere = pl.BlockSpec(memory_space=pl.ANY)
    dma = pltpu.SemaphoreType.DMA
    scratch = [pltpu.VMEM(whole, BF16) for _ in range(4)]
    scratch += [pltpu.VMEM(whole, BF16) for _ in range(2)]
    scratch += [
        pltpu.VMEM((heads, nblk, 3, block // 2, block // 2), BF16),
        pltpu.VMEM(whole, F32),
        pltpu.VMEM(whole, F32),
        pltpu.VMEM(whole, BF16),
        pltpu.VMEM(whole, F32),
    ]
    scratch += [pltpu.VMEM(whole, BF16) for _ in range(4)]
    scratch += [
        pltpu.VMEM((heads, nblk, PAY, E), F32),
        pltpu.VMEM((heads, nblk, PAY, E), F32),
        pltpu.VMEM((heads, nblk, E, 2 * E), BF16),
        pltpu.VMEM((2, heads, PAY, E), F32),
        pltpu.VMEM((2, half, PAY, E), F32),
        pltpu.VMEM((2, stages, half, PAY, E), F32),
        pltpu.VMEM((2, stages, half, PAY, E), F32),
        pltpu.VMEM((2, half, PAY, E), F32),
        pltpu.VMEM((2, heads, PAY, E), F32),
        pltpu.VMEM((nblk, 2, block), F32),
        pltpu.VMEM((nblk, n_head - 1, 2, block), F32),
        pltpu.VMEM((nblk, 2, block, E), F32),
        dma((4, heads)),
        dma((4, heads)),
        dma((2, half)),
        dma((2, half)),
        dma((2, stages, half)),
        dma((2, stages, half)),
        dma((2, half)),
        dma((2, half)),
        dma((nblk, n_head - 1)),
        dma((nblk, n_head - 1)),
    ]
    out = jax.ShapeDtypeStruct((rows, width), BF16)
    return pl.pallas_call(
        functools.partial(kernel, dims),
        out_shape=(out,) * 4,
        in_specs=[anywhere, anywhere, anywhere, pl.BlockSpec(memory_space=pltpu.VMEM), anywhere],
        out_specs=(anywhere,) * 4,
        scratch_shapes=scratch,
        compiler_params=pltpu.CompilerParams(
            collective_id=0, has_side_effects=True, vmem_limit_bytes=60 * 1024 * 1024
        ),
        cost_estimate=pl.CostEstimate(
            flops=16 * rows * block * width, bytes_accessed=16 * rows * width,
            transcendentals=4 * rows * width,
        ),
    )(queries, keys, values, gain.reshape(heads, E), cotangent)


def solution(mesh):
    sizes = tuple(mesh.shape[name] for name in ("seqin", "seqout", "head"))
    rows = P(("seqin", "seqout"), "head")
    return jax.shard_map(
        functools.partial(shards, sizes),
        mesh=mesh,
        in_specs=(rows, rows, rows, P("head"), rows),
        out_specs=(rows,) * 4,
        check_vma=False,
    )
```

```python
import functools

import jax
import jax.numpy as jnp
from jax import lax
from jax.experimental import pallas as pl
from jax.experimental.pallas import tpu as pltpu
from jax.sharding import PartitionSpec as P

E = 128
BLOCK = 512
NORM = E
PAY = E + 8
F32 = jnp.float32
BF16 = jnp.bfloat16
VMEM_A = 34 * 1024 * 1024
VMEM_B = 8 * 1024 * 1024
MESH = pl.DeviceIdType.MESH


def features(x):
    xf = x.astype(F32)
    return jnp.where(xf > 0, xf + 1.0, jnp.exp(jnp.minimum(xf, 0.0))).astype(BF16)


def slope(x):
    return jnp.exp(jnp.minimum(x.astype(F32), 0.0))


def dot(a, b, ca=1, cb=0):
    return lax.dot_general(a, b, (((ca,), (cb,)), ((), ())), preferred_element_type=F32)


def split(x):
    hi = x.astype(BF16)
    return hi, (x - hi.astype(F32)).astype(BF16)


def each(n, body):
    def step(j, carry):
        body(j)
        return carry
    lax.fori_loop(0, n, step, 0)


def kernel(dims, q_hbm, k_hbm, v_hbm, gain_ref, c_hbm, om, oq, kv, vv, fk, att, dvp, lat,
           qv, cv, fq, wts, den, gn, kvb, rvb, sh, tot, r0, tx, rx, fin, pfx, stat, stat_in, scl,
           in_sem, s0, q0, sx, rxs, s2, q2, ss, rs):
    heads, nblk, block, n_in, n_out, n_head, width = dims
    half = heads // 2
    tile = block // 2
    n_seq = n_in * n_out
    nchips = n_seq // 2
    stages = nchips.bit_length() - 1
    a_in, a_out, a_head = lax.axis_index("seqin"), lax.axis_index("seqout"), lax.axis_index("head")
    me = a_in * n_out + a_out
    core = lax.rem(me, 2)
    mine = core * half
    theirs = (1 - core) * half

    def bit(m):
        return lax.rem(lax.div(me, m), 2)

    def peer(m):
        other = me + m - 2 * m * bit(m)
        return (lax.div(other, n_out), lax.rem(other, n_out), a_head)

    def zpeer(d):
        return (a_in, a_out, lax.rem(a_head + d, n_head))

    def fetch(array, h):
        src, dst = ((k_hbm, kv), (v_hbm, vv), (q_hbm, qv), (c_hbm, cv))[array]
        cols = pl.ds(pl.multiple_of(h * E, E), E)
        return pltpu.make_async_copy(src.at[:, cols], dst.at[h], in_sem.at[array, h])

    def order(j):
        return lax.rem(theirs + j, heads)

    def start_kv(j):
        fetch(0, order(j)).start()
        fetch(1, order(j)).start()

    def start_qc(h):
        fetch(2, h).start()
        fetch(3, h).start()

    each(heads, start_kv)
    each(heads, start_qc)

    barrier = pltpu.get_barrier_semaphore()
    masks = [1 << s for s in range(stages + 1)]
    for m in masks:
        pl.semaphore_signal(barrier, inc=1, device_id=peer(m), device_id_type=MESH)
    for d in range(1, n_head):
        pl.semaphore_signal(barrier, inc=1, device_id=zpeer(d), device_id_type=MESH)

    def swap(dirn, j):
        return pltpu.make_async_remote_copy(
            src_ref=tot.at[dirn, theirs + j], dst_ref=r0.at[dirn, j],
            send_sem=s0.at[dirn, j], recv_sem=q0.at[dirn, j],
            device_id=peer(1), device_id_type=MESH)

    def hop(dirn, s, j):
        return pltpu.make_async_remote_copy(
            src_ref=tx.at[dirn, s, j], dst_ref=rx.at[dirn, s, j],
            send_sem=sx.at[dirn, s, j], recv_sem=rxs.at[dirn, s, j],
            device_id=peer(2 << s), device_id_type=MESH)

    def back(dirn, j):
        return pltpu.make_async_remote_copy(
            src_ref=fin.at[dirn, j], dst_ref=pfx.at[dirn, mine + j],
            send_sem=s2.at[dirn, j], recv_sem=q2.at[dirn, j],
            device_id=peer(1), device_id_type=MESH)

    def back_in(dirn, j):
        return pltpu.make_async_remote_copy(
            src_ref=fin.at[dirn, j], dst_ref=pfx.at[dirn, theirs + j],
            send_sem=s2.at[dirn, j], recv_sem=q2.at[dirn, j],
            device_id=peer(1), device_id_type=MESH)

    def chip_total(dirn):
        def body(j):
            swap(dirn, j).wait_recv()
            tx[dirn, 0, j] = tot[dirn, mine + j] + r0[dirn, j]
            hop(dirn, 0, j).start()
        each(half, body)

    def hop_on(dirn, s):
        def body(j):
            hop(dirn, s, j).wait_recv()
            if s + 1 < stages:
                tx[dirn, s + 1, j] = tx[dirn, s, j] + rx[dirn, s, j]
                hop(dirn, s + 1, j).start()
                return
            total = jnp.zeros((PAY, E), F32)
            for i in range(stages):
                before = bit(2 << i) == 1 - dirn
                total = total + jnp.where(before, rx[dirn, i, j], 0.0)
            near = core == dirn
            own, other = tot[dirn, mine + j], r0[dirn, j]
            fin[dirn, j] = total + jnp.where(near, own, 0.0)
            pfx[dirn, mine + j] = total + jnp.where(near, 0.0, other)
            back(dirn, j).start()
        each(half, body)

    def arrive(dirn):
        each(half, lambda j: back_in(dirn, j).wait_recv())

    def drain(dirn):
        def body(j):
            swap(dirn, j).wait_send()
            for s in range(stages):
                hop(dirn, s, j).wait_send()
            back(dirn, j).wait_send()
        each(half, body)

    def rows(b):
        return pl.ds(b * block, block)

    def key_sums(h):
        fetch(0, h).wait()
        fetch(1, h).wait()
        total = jnp.zeros((PAY, E), F32)
        for b in range(nblk):
            f = features(kv[h, rows(b), :])
            fk[h, rows(b), :] = f
            state = dot(f, vv[h, rows(b), :], 0, 0)
            norm = jnp.sum(f.astype(F32), axis=0, keepdims=True)
            part = jnp.concatenate([state, jnp.broadcast_to(norm, (8, E))], axis=0)
            kvb[h, b] = part
            total = total + part
        tot[0, h] = total

    def causal():
        return (lax.broadcasted_iota(jnp.int32, (tile, tile), 0)
                >= lax.broadcasted_iota(jnp.int32, (tile, tile), 1))

    def forward_local(h):
        fetch(2, h).wait()
        keep = causal()
        ones = jnp.ones((block, E), BF16)
        for b in range(nblk):
            base = b * block
            f = features(qv[h, rows(b), :])
            fq[h, rows(b), :] = f
            g = fk[h, rows(b), :]
            va = jnp.concatenate([vv[h, rows(b), :], ones], axis=1)
            top = jnp.where(keep, dot(f[:tile], g[:tile], 1, 1), 0.0).astype(BF16)
            low = dot(f[tile:], g, 1, 1)
            left = low[:, :tile].astype(BF16)
            right = jnp.where(keep, low[:, tile:], 0.0).astype(BF16)
            wts[h, b, 0] = top
            wts[h, b, 1] = left
            wts[h, b, 2] = right
            up = dot(top, va[:tile])
            down = dot(jnp.concatenate([left, right], axis=1), va)
            att[h, pl.ds(base, tile), :] = up[:, :E]
            den[h, pl.ds(base, tile), :] = up[:, E:]
            att[h, pl.ds(base + tile, tile), :] = down[:, :E]
            den[h, pl.ds(base + tile, tile), :] = down[:, E:]

    def forward_state(b):
        def body(h, sums):
            sq, pr = sums
            if b == 0:
                fetch(3, h).wait()
            full = pfx[0, h]
            for a in range(b):
                full = full + kvb[h, a]
            hi, lo = split(full[:E])
            sh[h, b] = jnp.concatenate([hi, lo], axis=1)
            norm = jnp.transpose(jnp.broadcast_to(full[NORM:NORM + 1], (E, E)))
            nhi, nlo = split(norm)
            wide = jnp.concatenate([jnp.concatenate([hi, nhi], axis=1),
                                    jnp.concatenate([lo, nlo], axis=1)], axis=0)
            f = fq[h, rows(b), :]
            both = dot(jnp.concatenate([f, f], axis=1), wide)
            inv = 1.0 / (den[h, rows(b), :] + both[:, E:])
            out = (att[h, rows(b), :] + both[:, :E]) * inv
            den[h, rows(b), :] = inv
            att[h, rows(b), :] = out
            w = cv[h, rows(b), :].astype(F32) * gain_ref[pl.ds(h, 1), :]
            return sq + out * out, pr + w * out
        zero = jnp.zeros((block, E), F32)
        sq, pr = lax.fori_loop(0, heads, body, (zero, zero))
        stat[b, 0:1, :] = jnp.sum(jnp.transpose(sq), axis=0, keepdims=True)
        stat[b, 1:2, :] = jnp.sum(jnp.transpose(pr), axis=0, keepdims=True)

    def share(b, d):
        return pltpu.make_async_remote_copy(
            src_ref=stat.at[b], dst_ref=stat_in.at[b, d - 1],
            send_sem=ss.at[b, d - 1], recv_sem=rs.at[b, d - 1],
            device_id=zpeer(d), device_id_type=MESH)

    def scales(b):
        for d in range(1, n_head):
            share(b, d).wait_recv()
        total = stat[b]
        for d in range(1, n_head):
            total = total + stat_in[b, d - 1]
        scale = lax.rsqrt(total[0:1] / width + 1e-06)
        pull = scale * scale * scale * total[1:2] / width
        scl[b, 0] = jnp.transpose(jnp.broadcast_to(scale, (E, block)))
        scl[b, 1] = jnp.transpose(jnp.broadcast_to(pull, (E, block)))

    def gradient(h):
        total = jnp.zeros((PAY, E), F32)
        gain = gain_ref[pl.ds(h, 1), :]
        for b in range(nblk):
            scale, pull = scl[b, 0], scl[b, 1]
            out, inv = att[h, rows(b), :], den[h, rows(b), :]
            sg = scale * gain
            om[h, rows(b), :] = (out * sg).astype(BF16)
            d = sg * cv[h, rows(b), :].astype(F32) - out * pull
            g = (d * inv).astype(BF16)
            gd = -jnp.sum(d * out, axis=1, keepdims=True) * inv
            gn[h, rows(b), :] = g
            den[h, rows(b), :] = gd
            f = fq[h, rows(b), :]
            later = dot(f, g, 0, 0)
            lden = jnp.sum(gd * f.astype(F32), axis=0, keepdims=True)
            part = jnp.concatenate([later, jnp.broadcast_to(lden, (8, E))], axis=0)
            rvb[h, b] = part
            total = total + part
        tot[1, h] = total

    def backward_local(h):
        keep = causal()
        for b in range(nblk):
            base = b * block
            f, k, v, g = fq[h, rows(b), :], fk[h, rows(b), :], vv[h, rows(b), :], gn[h, rows(b), :]
            gd = den[h, rows(b), :]
            gw = jnp.concatenate([gd] * (tile // E), axis=1)
            top = jnp.where(keep, dot(g[:tile], v[:tile], 1, 1) + gw[:tile], 0.0).astype(BF16)
            low = dot(g[tile:], v, 1, 1)
            left = (low[:, :tile] + gw[tile:]).astype(BF16)
            right = jnp.where(keep, low[:, tile:] + gw[tile:], 0.0).astype(BF16)
            norm = pfx[0, h, NORM:NORM + 1, :]
            for a in range(b):
                norm = norm + kvb[h, a, NORM:NORM + 1, :]
            far = dot(jnp.concatenate([g, g], axis=1), sh[h, b], 1, 1) + gd * norm
            up = dot(top, k[:tile]) + far[:tile]
            down = dot(jnp.concatenate([left, right], axis=1), k) + far[tile:]
            sl = slope(qv[h, rows(b), :])
            oq[h, pl.ds(base, tile), :] = (up * sl[:tile]).astype(BF16)
            oq[h, pl.ds(base + tile, tile), :] = (down * sl[tile:]).astype(BF16)
            att[h, pl.ds(base, tile), :] = dot(jnp.concatenate([top, left], axis=0), f, 0, 0)
            att[h, pl.ds(base + tile, tile), :] = dot(right, f[tile:], 0, 0)
            first = jnp.concatenate([wts[h, b, 0], wts[h, b, 1]], axis=0)
            dvp[h, pl.ds(base, tile), :] = dot(first, g, 0, 0)
            dvp[h, pl.ds(base + tile, tile), :] = dot(wts[h, b, 2], g[tile:], 0, 0)

    def later_sums(h):
        full = pfx[1, h]
        for b in reversed(range(nblk)):
            lat[h, b] = full
            full = full + rvb[h, b]

    def middle(dirn, local):
        chip_total(dirn)
        per = heads // (stages + 1)
        at = 0
        for s in range(stages):
            low, count = at, per
            at += per
            each(count, lambda j, low=low: local(low + j))
            hop_on(dirn, s)
        each(heads - at, lambda j: local(at + j))
        arrive(dirn)

    def theirs_first(dirn, body):
        def one(j):
            body(theirs + j)
            swap(dirn, j).start()
        each(half, one)
        each(half, lambda j: body(mine + j))

    greeted = len(masks) + n_head - 1

    def one_ready(j):
        key_sums(theirs + j)

    each(half, one_ready)
    pl.semaphore_wait(barrier, greeted)
    each(half, lambda j: swap(0, j).start())
    each(half, lambda j: key_sums(mine + j))
    middle(0, forward_local)
    for b in range(nblk):
        forward_state(b)
        for d in range(1, n_head):
            share(b, d).start()
    for b in range(nblk):
        scales(b)
    theirs_first(1, gradient)
    middle(1, backward_local)
    each(heads, later_sums)

    drain(0)
    drain(1)
    for b in range(nblk):
        for d in range(1, n_head):
            share(b, d).wait_send()


def last(dims, om, oq, kv, vv, fk, att, dvp, lat, mixed_hbm, gq_hbm, gk_hbm, gv_hbm,
         ok, ov, out_sem):
    heads, nblk, block = dims[:3]

    def put(array, h):
        src, dst = ((om, mixed_hbm), (oq, gq_hbm), (ok, gk_hbm), (ov, gv_hbm))[array]
        cols = pl.ds(pl.multiple_of(h * E, E), E)
        return pltpu.make_async_copy(src.at[h], dst.at[:, cols], out_sem.at[array, h])

    def ready(h):
        put(0, h).start()
        put(1, h).start()

    def backward_state(h):
        for b in range(nblk):
            rows = pl.ds(b * block, block)
            full = lat[h, b]
            hi, lo = split(full[:E])
            v, k = vv[h, rows, :], fk[h, rows, :]
            dk = dot(jnp.concatenate([v, v], axis=1), jnp.concatenate([hi, lo], axis=1), 1, 1)
            dk = dk + att[h, rows, :] + full[NORM:NORM + 1]
            ok[h, rows, :] = (dk * slope(kv[h, rows, :])).astype(BF16)
            dv = dot(jnp.concatenate([k, k], axis=1), jnp.concatenate([hi, lo], axis=0))
            ov[h, rows, :] = (dv + dvp[h, rows, :]).astype(BF16)
        put(2, h).start()
        put(3, h).start()

    def finish(h):
        for array in range(4):
            put(array, h).wait()

    each(heads, ready)
    each(heads, backward_state)
    each(heads, finish)


def shards(sizes, queries, keys, values, gain, cotangent):
    n_in, n_out, n_head = sizes
    rows, width = queries.shape
    heads = width // E
    block = min(BLOCK, rows)
    nblk = rows // block
    half = heads // 2
    stages = max((n_in * n_out // 2).bit_length() - 1, 1)
    dims = (heads, nblk, block, n_in, n_out, n_head, width * n_head)
    whole = (heads, rows, E)
    anywhere = pl.BlockSpec(memory_space=pl.ANY)
    dma = pltpu.SemaphoreType.DMA
    half16, full32 = pltpu.VMEM(whole, BF16), pltpu.VMEM(whole, F32)
    held = (half16,) * 5 + (full32,) * 2 + (pltpu.VMEM((heads, nblk, PAY, E), F32),)
    scratch = [
        half16,
        half16,
        half16,
        pltpu.VMEM((heads, nblk, 3, block // 2, block // 2), BF16),
        full32,
        half16,
        pltpu.VMEM((heads, nblk, PAY, E), F32),
        pltpu.VMEM((heads, nblk, PAY, E), F32),
        pltpu.VMEM((heads, nblk, E, 2 * E), BF16),
        pltpu.VMEM((2, heads, PAY, E), F32),
        pltpu.VMEM((2, half, PAY, E), F32),
        pltpu.VMEM((2, stages, half, PAY, E), F32),
        pltpu.VMEM((2, stages, half, PAY, E), F32),
        pltpu.VMEM((2, half, PAY, E), F32),
        pltpu.VMEM((2, heads, PAY, E), F32),
        pltpu.VMEM((nblk, 2, block), F32),
        pltpu.VMEM((nblk, n_head - 1, 2, block), F32),
        pltpu.VMEM((nblk, 2, block, E), F32),
        dma((4, heads)),
        dma((2, half)),
        dma((2, half)),
        dma((2, stages, half)),
        dma((2, stages, half)),
        dma((2, half)),
        dma((2, half)),
        dma((nblk, n_head - 1)),
        dma((nblk, n_head - 1)),
    ]
    inside = pl.BlockSpec(memory_space=pltpu.VMEM)
    kept = pl.pallas_call(
        functools.partial(kernel, dims),
        out_shape=held,
        in_specs=[anywhere, anywhere, anywhere, inside, anywhere],
        out_specs=(inside,) * len(held),
        scratch_shapes=scratch,
        compiler_params=pltpu.CompilerParams(
            collective_id=0, has_side_effects=True, vmem_limit_bytes=VMEM_A
        ),
        cost_estimate=pl.CostEstimate(
            flops=16 * rows * block * width, bytes_accessed=8 * rows * width,
            transcendentals=4 * rows * width,
        ),
    )(queries, keys, values, gain.reshape(heads, E), cotangent)
    out = jax.ShapeDtypeStruct((rows, width), BF16)
    return pl.pallas_call(
        functools.partial(last, dims),
        out_shape=(out,) * 4,
        in_specs=[inside] * len(held),
        out_specs=(anywhere,) * 4,
        scratch_shapes=[half16, half16, dma((4, heads))],
        compiler_params=pltpu.CompilerParams(vmem_limit_bytes=VMEM_B),
        cost_estimate=pl.CostEstimate(
            flops=4 * rows * 2 * E * width, bytes_accessed=8 * rows * width,
            transcendentals=rows * width,
        ),
    )(*kept)


def solution(mesh):
    sizes = tuple(mesh.shape[name] for name in ("seqin", "seqout", "head"))
    rows = P(("seqin", "seqout"), "head")
    return jax.shard_map(
        functools.partial(shards, sizes),
        mesh=mesh,
        in_specs=(rows, rows, rows, P("head"), rows),
        out_specs=(rows,) * 4,
        check_vma=False,
    )
```

```python
import functools

import jax
import jax.numpy as jnp
from jax import lax
from jax.experimental import pallas as pl
from jax.experimental.pallas import tpu as pltpu
from jax.sharding import PartitionSpec as P

E = 128
BLOCK = 512
NORM = E
PAY = E + 8
F32 = jnp.float32
BF16 = jnp.bfloat16
VMEM_A = 34 * 1024 * 1024
VMEM_B = 8 * 1024 * 1024
MESH = pl.DeviceIdType.MESH


def features(x):
    xf = x.astype(F32)
    return jnp.where(xf > 0, xf + 1.0, jnp.exp(jnp.minimum(xf, 0.0))).astype(BF16)


def slope(x):
    return jnp.exp(jnp.minimum(x.astype(F32), 0.0))


def dot(a, b, ca=1, cb=0):
    return lax.dot_general(a, b, (((ca,), (cb,)), ((), ())), preferred_element_type=F32)


def split(x):
    hi = x.astype(BF16)
    return hi, (x - hi.astype(F32)).astype(BF16)


def each(n, body):
    def step(j, carry):
        body(j)
        return carry
    lax.fori_loop(0, n, step, 0)


def kernel(dims, q_hbm, k_hbm, v_hbm, g_hbm, c_hbm, om, oq, kv, vv, fk, att, dvp, lat,
           qv, cv, fq, wts, den, gn, kvb, rvb, sh, tot, r0, tx, rx, fin, pfx, stat, stat_in, scl,
           gain_ref, gain_sem, in_sem, s0, q0, sx, rxs, s2, q2, ss, rs):
    heads, nblk, block, n_in, n_out, n_head, width = dims
    half = heads // 2
    tile = block // 2
    n_seq = n_in * n_out
    nchips = n_seq // 2
    stages = nchips.bit_length() - 1
    a_in, a_out, a_head = lax.axis_index("seqin"), lax.axis_index("seqout"), lax.axis_index("head")
    me = a_in * n_out + a_out
    core = lax.rem(me, 2)
    mine = core * half
    theirs = (1 - core) * half

    def bit(m):
        return lax.rem(lax.div(me, m), 2)

    def peer(m):
        other = me + m - 2 * m * bit(m)
        return (lax.div(other, n_out), lax.rem(other, n_out), a_head)

    def zpeer(d):
        return (a_in, a_out, lax.rem(a_head + d, n_head))

    def fetch(array, h):
        src, dst = ((k_hbm, kv), (v_hbm, vv), (q_hbm, qv), (c_hbm, cv))[array]
        cols = pl.ds(pl.multiple_of(h * E, E), E)
        return pltpu.make_async_copy(src.at[:, cols], dst.at[h], in_sem.at[array, h])

    def start_kv(j):
        for h in (theirs + j, mine + j):
            fetch(0, h).start()
            fetch(1, h).start()

    def start_qc(h):
        fetch(2, h).start()

    each(half, start_kv)
    each(heads, start_qc)
    each(heads, lambda h: fetch(3, h).start())
    gain_copy = pltpu.make_async_copy(g_hbm, gain_ref, gain_sem)
    gain_copy.start()

    barrier = pltpu.get_barrier_semaphore()
    masks = [1 << s for s in range(stages + 1)]
    for m in masks:
        pl.semaphore_signal(barrier, inc=1, device_id=peer(m), device_id_type=MESH)
    for d in range(1, n_head):
        pl.semaphore_signal(barrier, inc=1, device_id=zpeer(d), device_id_type=MESH)

    def swap(dirn, j):
        return pltpu.make_async_remote_copy(
            src_ref=tot.at[dirn, theirs + j], dst_ref=r0.at[dirn, j],
            send_sem=s0.at[dirn, j], recv_sem=q0.at[dirn, j],
            device_id=peer(1), device_id_type=MESH)

    def hop(dirn, s, j):
        return pltpu.make_async_remote_copy(
            src_ref=tx.at[dirn, s, j], dst_ref=rx.at[dirn, s, j],
            send_sem=sx.at[dirn, s, j], recv_sem=rxs.at[dirn, s, j],
            device_id=peer(2 << s), device_id_type=MESH)

    def back(dirn, j):
        return pltpu.make_async_remote_copy(
            src_ref=fin.at[dirn, j], dst_ref=pfx.at[dirn, mine + j],
            send_sem=s2.at[dirn, j], recv_sem=q2.at[dirn, j],
            device_id=peer(1), device_id_type=MESH)

    def back_in(dirn, j):
        return pltpu.make_async_remote_copy(
            src_ref=fin.at[dirn, j], dst_ref=pfx.at[dirn, theirs + j],
            send_sem=s2.at[dirn, j], recv_sem=q2.at[dirn, j],
            device_id=peer(1), device_id_type=MESH)

    def chip_total(dirn, j):
        swap(dirn, j).wait_recv()
        tx[dirn, 0, j] = tot[dirn, mine + j] + r0[dirn, j]
        hop(dirn, 0, j).start()

    def hop_on(dirn, s, j):
        hop(dirn, s, j).wait_recv()
        if s + 1 < stages:
            tx[dirn, s + 1, j] = tx[dirn, s, j] + rx[dirn, s, j]
            hop(dirn, s + 1, j).start()
            return
        total = jnp.zeros((PAY, E), F32)
        for i in range(stages):
            before = bit(2 << i) == 1 - dirn
            total = total + jnp.where(before, rx[dirn, i, j], 0.0)
        near = core == dirn
        own, other = tot[dirn, mine + j], r0[dirn, j]
        fin[dirn, j] = total + jnp.where(near, own, 0.0)
        pfx[dirn, mine + j] = total + jnp.where(near, 0.0, other)
        back(dirn, j).start()

    def arrive(dirn):
        each(half, lambda j: back_in(dirn, j).wait_recv())

    def drain(dirn):
        def body(j):
            swap(dirn, j).wait_send()
            for s in range(stages):
                hop(dirn, s, j).wait_send()
            back(dirn, j).wait_send()
        each(half, body)

    def rows(b):
        return pl.ds(b * block, block)

    def key_sums(h):
        fetch(0, h).wait()
        fetch(1, h).wait()
        total = jnp.zeros((PAY, E), F32)
        for b in range(nblk):
            f = features(kv[h, rows(b), :])
            fk[h, rows(b), :] = f
            state = dot(f, vv[h, rows(b), :], 0, 0)
            norm = jnp.sum(f.astype(F32), axis=0, keepdims=True)
            part = jnp.concatenate([state, jnp.broadcast_to(norm, (8, E))], axis=0)
            kvb[h, b] = part
            total = total + part
        tot[0, h] = total

    def causal():
        return (lax.broadcasted_iota(jnp.int32, (tile, tile), 0)
                >= lax.broadcasted_iota(jnp.int32, (tile, tile), 1))

    def forward_local(h):
        fetch(2, h).wait()
        keep = causal()
        ones = jnp.ones((block, E), BF16)
        for b in range(nblk):
            base = b * block
            f = features(qv[h, rows(b), :])
            fq[h, rows(b), :] = f
            g = fk[h, rows(b), :]
            va = jnp.concatenate([vv[h, rows(b), :], ones], axis=1)
            top = jnp.where(keep, dot(f[:tile], g[:tile], 1, 1), 0.0).astype(BF16)
            low = dot(f[tile:], g, 1, 1)
            left = low[:, :tile].astype(BF16)
            right = jnp.where(keep, low[:, tile:], 0.0).astype(BF16)
            wts[h, b, 0] = top
            wts[h, b, 1] = left
            wts[h, b, 2] = right
            up = dot(top, va[:tile])
            down = dot(jnp.concatenate([left, right], axis=1), va)
            att[h, pl.ds(base, tile), :] = up[:, :E]
            den[h, pl.ds(base, tile), :] = up[:, E:]
            att[h, pl.ds(base + tile, tile), :] = down[:, :E]
            den[h, pl.ds(base + tile, tile), :] = down[:, E:]

    def forward_state(b):
        def body(h, sums):
            sq, pr = sums
            if b == 0:
                fetch(3, h).wait()
            full = pfx[0, h]
            for a in range(b):
                full = full + kvb[h, a]
            hi, lo = split(full[:E])
            sh[h, b] = jnp.concatenate([hi, lo], axis=1)
            norm = jnp.transpose(jnp.broadcast_to(full[NORM:NORM + 1], (E, E)))
            nhi, nlo = split(norm)
            wide = jnp.concatenate([jnp.concatenate([hi, nhi], axis=1),
                                    jnp.concatenate([lo, nlo], axis=1)], axis=0)
            f = fq[h, rows(b), :]
            both = dot(jnp.concatenate([f, f], axis=1), wide)
            inv = 1.0 / (den[h, rows(b), :] + both[:, E:])
            out = (att[h, rows(b), :] + both[:, :E]) * inv
            den[h, rows(b), :] = inv
            att[h, rows(b), :] = out
            w = cv[h, rows(b), :].astype(F32) * gain_ref[pl.ds(h, 1), :]
            return sq + out * out, pr + w * out
        zero = jnp.zeros((block, E), F32)
        sq, pr = lax.fori_loop(0, heads, body, (zero, zero))
        stat[b, 0:1, :] = jnp.sum(jnp.transpose(sq), axis=0, keepdims=True)
        stat[b, 1:2, :] = jnp.sum(jnp.transpose(pr), axis=0, keepdims=True)

    def share(b, d):
        return pltpu.make_async_remote_copy(
            src_ref=stat.at[b], dst_ref=stat_in.at[b, d - 1],
            send_sem=ss.at[b, d - 1], recv_sem=rs.at[b, d - 1],
            device_id=zpeer(d), device_id_type=MESH)

    def scales(b):
        for d in range(1, n_head):
            share(b, d).wait_recv()
        total = stat[b]
        for d in range(1, n_head):
            total = total + stat_in[b, d - 1]
        scale = lax.rsqrt(total[0:1] / width + 1e-06)
        pull = scale * scale * scale * total[1:2] / width
        scl[b, 0] = jnp.transpose(jnp.broadcast_to(scale, (E, block)))
        scl[b, 1] = jnp.transpose(jnp.broadcast_to(pull, (E, block)))

    def gradient(b, h):
        gain = gain_ref[pl.ds(h, 1), :]
        scale, pull = scl[b, 0], scl[b, 1]
        out, inv = att[h, rows(b), :], den[h, rows(b), :]
        sg = scale * gain
        om[h, rows(b), :] = (out * sg).astype(BF16)
        d = sg * cv[h, rows(b), :].astype(F32) - out * pull
        g = (d * inv).astype(BF16)
        gd = -jnp.sum(d * out, axis=1, keepdims=True) * inv
        gn[h, rows(b), :] = g
        den[h, rows(b), :] = gd
        f = fq[h, rows(b), :]
        later = dot(f, g, 0, 0)
        lden = jnp.sum(gd * f.astype(F32), axis=0, keepdims=True)
        part = jnp.concatenate([later, jnp.broadcast_to(lden, (8, E))], axis=0)
        rvb[h, b] = part
        tot[1, h] = tot[1, h] + part if b else part

    def backward_local(h):
        keep = causal()
        for b in range(nblk):
            base = b * block
            f, k, v, g = fq[h, rows(b), :], fk[h, rows(b), :], vv[h, rows(b), :], gn[h, rows(b), :]
            gd = den[h, rows(b), :]
            gw = jnp.concatenate([gd] * (tile // E), axis=1)
            top = jnp.where(keep, dot(g[:tile], v[:tile], 1, 1) + gw[:tile], 0.0).astype(BF16)
            low = dot(g[tile:], v, 1, 1)
            left = (low[:, :tile] + gw[tile:]).astype(BF16)
            right = jnp.where(keep, low[:, tile:] + gw[tile:], 0.0).astype(BF16)
            norm = pfx[0, h, NORM:NORM + 1, :]
            for a in range(b):
                norm = norm + kvb[h, a, NORM:NORM + 1, :]
            far = dot(jnp.concatenate([g, g], axis=1), sh[h, b], 1, 1) + gd * norm
            up = dot(top, k[:tile]) + far[:tile]
            down = dot(jnp.concatenate([left, right], axis=1), k) + far[tile:]
            sl = slope(qv[h, rows(b), :])
            oq[h, pl.ds(base, tile), :] = (up * sl[:tile]).astype(BF16)
            oq[h, pl.ds(base + tile, tile), :] = (down * sl[tile:]).astype(BF16)
            att[h, pl.ds(base, tile), :] = dot(jnp.concatenate([top, left], axis=0), f, 0, 0)
            att[h, pl.ds(base + tile, tile), :] = dot(right, f[tile:], 0, 0)
            first = jnp.concatenate([wts[h, b, 0], wts[h, b, 1]], axis=0)
            dvp[h, pl.ds(base, tile), :] = dot(first, g, 0, 0)
            dvp[h, pl.ds(base + tile, tile), :] = dot(wts[h, b, 2], g[tile:], 0, 0)

    def later_sums(h):
        full = pfx[1, h]
        for b in reversed(range(nblk)):
            lat[h, b] = full
            full = full + rvb[h, b]

    def sums(dirn, body, greet=None):
        body(theirs)
        if greet is not None:
            greet()
        swap(dirn, 0).start()

        def step(j):
            body(mine + j)

            @pl.when(j < half - 1)
            def _():
                body(theirs + j + 1)
                swap(dirn, j + 1).start()
            chip_total(dirn, j)
        each(half, step)

    def middle(dirn, local, slot):
        events = sorted((slot(s, j), s, j) for s in range(stages) for j in range(half))

        def step(h):
            local(h)
            for at, s, j in events:
                if at < heads:
                    @pl.when(h == at)
                    def _(s=s, j=j):
                        hop_on(dirn, s, j)
        each(heads, step)
        for at, s, j in events:
            if at >= heads:
                hop_on(dirn, s, j)
        arrive(dirn)

    greeted = len(masks) + n_head - 1
    sums(0, key_sums, lambda: pl.semaphore_wait(barrier, greeted))
    middle(0, forward_local, lambda s, j: 1 + (3 * j) // 2 + 4 * s)
    gain_copy.wait()
    for b in range(nblk):
        forward_state(b)
        for d in range(1, n_head):
            share(b, d).start()
    for b in range(nblk - 1):
        scales(b)
        each(heads, functools.partial(gradient, b))
    scales(nblk - 1)
    sums(1, functools.partial(gradient, nblk - 1))
    middle(1, backward_local, lambda s, j: j + 2 * s)
    each(heads, later_sums)

    drain(0)
    drain(1)
    for b in range(nblk):
        for d in range(1, n_head):
            share(b, d).wait_send()


def last(dims, om, oq, kv, vv, fk, att, dvp, lat, mixed_hbm, gq_hbm, gk_hbm, gv_hbm,
         ok, ov, out_sem):
    heads, nblk, block = dims[:3]

    def put(array, h):
        src, dst = ((om, mixed_hbm), (oq, gq_hbm), (ok, gk_hbm), (ov, gv_hbm))[array]
        cols = pl.ds(pl.multiple_of(h * E, E), E)
        return pltpu.make_async_copy(src.at[h], dst.at[:, cols], out_sem.at[array, h])

    def ready(h):
        put(0, h).start()
        put(1, h).start()

    def backward_state(h):
        for b in range(nblk):
            rows = pl.ds(b * block, block)
            full = lat[h, b]
            hi, lo = split(full[:E])
            v, k = vv[h, rows, :], fk[h, rows, :]
            dk = dot(jnp.concatenate([v, v], axis=1), jnp.concatenate([hi, lo], axis=1), 1, 1)
            dk = dk + att[h, rows, :] + full[NORM:NORM + 1]
            ok[h, rows, :] = (dk * slope(kv[h, rows, :])).astype(BF16)
            dv = dot(jnp.concatenate([k, k], axis=1), jnp.concatenate([hi, lo], axis=0))
            ov[h, rows, :] = (dv + dvp[h, rows, :]).astype(BF16)
        put(2, h).start()
        put(3, h).start()

    def finish(h):
        for array in range(4):
            put(array, h).wait()

    each(heads, ready)
    each(heads, backward_state)
    each(heads, finish)


def shards(sizes, queries, keys, values, gain, cotangent):
    n_in, n_out, n_head = sizes
    rows, width = queries.shape
    heads = width // E
    block = min(BLOCK, rows)
    nblk = rows // block
    half = heads // 2
    stages = max((n_in * n_out // 2).bit_length() - 1, 1)
    dims = (heads, nblk, block, n_in, n_out, n_head, width * n_head)
    whole = (heads, rows, E)
    anywhere = pl.BlockSpec(memory_space=pl.ANY)
    dma = pltpu.SemaphoreType.DMA
    half16, full32 = pltpu.VMEM(whole, BF16), pltpu.VMEM(whole, F32)
    held = (half16,) * 5 + (full32,) * 2 + (pltpu.VMEM((heads, nblk, PAY, E), F32),)
    scratch = [
        half16,
        half16,
        half16,
        pltpu.VMEM((heads, nblk, 3, block // 2, block // 2), BF16),
        full32,
        half16,
        pltpu.VMEM((heads, nblk, PAY, E), F32),
        pltpu.VMEM((heads, nblk, PAY, E), F32),
        pltpu.VMEM((heads, nblk, E, 2 * E), BF16),
        pltpu.VMEM((2, heads, PAY, E), F32),
        pltpu.VMEM((2, half, PAY, E), F32),
        pltpu.VMEM((2, stages, half, PAY, E), F32),
        pltpu.VMEM((2, stages, half, PAY, E), F32),
        pltpu.VMEM((2, half, PAY, E), F32),
        pltpu.VMEM((2, heads, PAY, E), F32),
        pltpu.VMEM((nblk, 2, block), F32),
        pltpu.VMEM((nblk, n_head - 1, 2, block), F32),
        pltpu.VMEM((nblk, 2, block, E), F32),
        pltpu.VMEM((heads, E), F32),
        dma,
        dma((4, heads)),
        dma((2, half)),
        dma((2, half)),
        dma((2, stages, half)),
        dma((2, stages, half)),
        dma((2, half)),
        dma((2, half)),
        dma((nblk, n_head - 1)),
        dma((nblk, n_head - 1)),
    ]
    inside = pl.BlockSpec(memory_space=pltpu.VMEM)
    kept = pl.pallas_call(
        functools.partial(kernel, dims),
        out_shape=held,
        in_specs=[pl.BlockSpec(memory_space=pltpu.MemorySpace.HBM)] * 5,
        out_specs=(inside,) * len(held),
        scratch_shapes=scratch,
        compiler_params=pltpu.CompilerParams(
            collective_id=0, has_side_effects=True, vmem_limit_bytes=VMEM_A
        ),
        cost_estimate=pl.CostEstimate(
            flops=16 * rows * block * width, bytes_accessed=8 * rows * width,
            transcendentals=4 * rows * width,
        ),
    )(queries, keys, values, gain.reshape(heads, E), cotangent)
    out = jax.ShapeDtypeStruct((rows, width), BF16)
    return pl.pallas_call(
        functools.partial(last, dims),
        out_shape=(out,) * 4,
        in_specs=[inside] * len(held),
        out_specs=(anywhere,) * 4,
        scratch_shapes=[half16, half16, dma((4, heads))],
        compiler_params=pltpu.CompilerParams(vmem_limit_bytes=VMEM_B),
        cost_estimate=pl.CostEstimate(
            flops=4 * rows * 2 * E * width, bytes_accessed=8 * rows * width,
            transcendentals=rows * width,
        ),
    )(*kept)


def solution(mesh):
    sizes = tuple(mesh.shape[name] for name in ("seqin", "seqout", "head"))
    rows = P(("seqin", "seqout"), "head")
    return jax.shard_map(
        functools.partial(shards, sizes),
        mesh=mesh,
        in_specs=(rows, rows, rows, P("head"), rows),
        out_specs=(rows,) * 4,
        check_vma=False,
    )
```

```python
import functools

import jax
import jax.numpy as jnp
from jax import lax
from jax.experimental import pallas as pl
from jax.experimental.pallas import tpu as pltpu
from jax.sharding import PartitionSpec as P

E = 128
BLOCK = 256
NORM = E
PAY = E + 8
F32 = jnp.float32
BF16 = jnp.bfloat16
VMEM_A = 34 * 1024 * 1024
VMEM_B = 8 * 1024 * 1024
MESH = pl.DeviceIdType.MESH


def features(x):
    xf = x.astype(F32)
    return jnp.where(xf > 0, xf + 1.0, jnp.exp(jnp.minimum(xf, 0.0))).astype(BF16)


def slope(x):
    return jnp.exp(jnp.minimum(x.astype(F32), 0.0))


def dot(a, b, ca=1, cb=0):
    return lax.dot_general(a, b, (((ca,), (cb,)), ((), ())), preferred_element_type=F32)


def split(x):
    hi = x.astype(BF16)
    return hi, (x - hi.astype(F32)).astype(BF16)


def each(n, body):
    def step(j, carry):
        body(j)
        return carry
    lax.fori_loop(0, n, step, 0)


def kernel(dims, q_hbm, k_hbm, v_hbm, g_hbm, c_hbm, om, oq, kv, vv, fk, att, dvp, lat,
           qv, cv, fq, wts, den, gn, kvb, rvb, sh, tot, r0, tx, rx, fin, pfx, stat, stat_in, acc, nrm,
           gain_ref, gain_sem, in_sem, s0, q0, sx, rxs, s2, q2, ss, rs):
    heads, nblk, block, n_in, n_out, n_head, width = dims
    half = heads // 2
    n_seq = n_in * n_out
    nchips = n_seq // 2
    stages = nchips.bit_length() - 1
    a_in, a_out, a_head = lax.axis_index("seqin"), lax.axis_index("seqout"), lax.axis_index("head")
    me = a_in * n_out + a_out
    core = lax.rem(me, 2)
    mine = core * half
    theirs = (1 - core) * half

    def bit(m):
        return lax.rem(lax.div(me, m), 2)

    def peer(m):
        other = me + m - 2 * m * bit(m)
        return (lax.div(other, n_out), lax.rem(other, n_out), a_head)

    def zpeer(d):
        return (a_in, a_out, lax.rem(a_head + d, n_head))

    def fetch(array, h):
        src, dst = ((k_hbm, kv), (v_hbm, vv), (q_hbm, qv), (c_hbm, cv))[array]
        cols = pl.ds(pl.multiple_of(h * E, E), E)
        return pltpu.make_async_copy(src.at[:, cols], dst.at[h], in_sem.at[array, h])

    def start_kv(j):
        for h in (theirs + j, mine + j):
            fetch(0, h).start()
            fetch(1, h).start()

    def start_qc(h):
        fetch(2, h).start()

    each(half, start_kv)
    each(heads, start_qc)
    each(heads, lambda h: fetch(3, h).start())
    gain_copy = pltpu.make_async_copy(g_hbm, gain_ref, gain_sem)
    gain_copy.start()

    barrier = pltpu.get_barrier_semaphore()
    masks = [1 << s for s in range(stages + 1)]
    for m in masks:
        pl.semaphore_signal(barrier, inc=1, device_id=peer(m), device_id_type=MESH)
    for d in range(1, n_head):
        pl.semaphore_signal(barrier, inc=1, device_id=zpeer(d), device_id_type=MESH)

    def swap(dirn, j):
        return pltpu.make_async_remote_copy(
            src_ref=tot.at[dirn, theirs + j], dst_ref=r0.at[dirn, j],
            send_sem=s0.at[dirn, j], recv_sem=q0.at[dirn, j],
            device_id=peer(1), device_id_type=MESH)

    def hop(dirn, s, j):
        return pltpu.make_async_remote_copy(
            src_ref=tx.at[dirn, s, j], dst_ref=rx.at[dirn, s, j],
            send_sem=sx.at[dirn, s, j], recv_sem=rxs.at[dirn, s, j],
            device_id=peer(2 << s), device_id_type=MESH)

    def back(dirn, j):
        return pltpu.make_async_remote_copy(
            src_ref=fin.at[dirn, j], dst_ref=pfx.at[dirn, mine + j],
            send_sem=s2.at[dirn, j], recv_sem=q2.at[dirn, j],
            device_id=peer(1), device_id_type=MESH)

    def back_in(dirn, j):
        return pltpu.make_async_remote_copy(
            src_ref=fin.at[dirn, j], dst_ref=pfx.at[dirn, theirs + j],
            send_sem=s2.at[dirn, j], recv_sem=q2.at[dirn, j],
            device_id=peer(1), device_id_type=MESH)

    def chip_total(dirn, j):
        swap(dirn, j).wait_recv()
        tx[dirn, 0, j] = tot[dirn, mine + j] + r0[dirn, j]
        hop(dirn, 0, j).start()

    def hop_on(dirn, s, j):
        hop(dirn, s, j).wait_recv()
        if s + 1 < stages:
            tx[dirn, s + 1, j] = tx[dirn, s, j] + rx[dirn, s, j]
            hop(dirn, s + 1, j).start()
            return
        total = jnp.zeros((PAY, E), F32)
        for i in range(stages):
            before = bit(2 << i) == 1 - dirn
            total = total + jnp.where(before, rx[dirn, i, j], 0.0)
        near = core == dirn
        own, other = tot[dirn, mine + j], r0[dirn, j]
        fin[dirn, j] = total + jnp.where(near, own, 0.0)
        pfx[dirn, mine + j] = total + jnp.where(near, 0.0, other)
        back(dirn, j).start()

    def arrive(dirn):
        each(half, lambda j: back_in(dirn, j).wait_recv())

    def drain(dirn):
        def body(j):
            swap(dirn, j).wait_send()
            for s in range(stages):
                hop(dirn, s, j).wait_send()
            back(dirn, j).wait_send()
        each(half, body)

    def rows(b):
        return pl.ds(b * block, block)

    def key_sums(h):
        fetch(0, h).wait()
        fetch(1, h).wait()
        total = jnp.zeros((PAY, E), F32)
        for b in range(nblk):
            f = features(kv[h, rows(b), :])
            fk[h, rows(b), :] = f
            state = dot(f, vv[h, rows(b), :], 0, 0)
            norm = jnp.sum(f.astype(F32), axis=0, keepdims=True)
            part = jnp.concatenate([state, jnp.broadcast_to(norm, (8, E))], axis=0)
            kvb[h, b] = part
            total = total + part
        tot[0, h] = total

    def causal():
        return (lax.broadcasted_iota(jnp.int32, (block, block), 0)
                >= lax.broadcasted_iota(jnp.int32, (block, block), 1))

    def forward_local(h):
        fetch(2, h).wait()
        keep = causal()
        ones = jnp.ones((block, E), BF16)
        for b in range(nblk):
            f = features(qv[h, rows(b), :])
            fq[h, rows(b), :] = f
            w = jnp.where(keep, dot(f, fk[h, rows(b), :], 1, 1), 0.0).astype(BF16)
            wts[h, b] = w
            both = dot(w, jnp.concatenate([vv[h, rows(b), :], ones], axis=1))
            att[h, rows(b), :] = both[:, :E]
            den[h, rows(b), :] = both[:, E:]

    def forward_state(j):
        back_in(0, j).wait_recv()
        pair = (mine + j, theirs + j)
        full = []
        for h in pair:
            fetch(3, h).wait()
            full.append(pfx[0, h])
        for b in range(nblk):
            sq, pr = acc[0, rows(b), :], acc[1, rows(b), :]
            for i, h in enumerate(pair):
                hi, lo = split(full[i][:E])
                sh[h, b] = jnp.concatenate([hi, lo], axis=1)
                norm = full[i][NORM:NORM + 1]
                nrm[h, b] = jnp.broadcast_to(norm, (8, E))
                nhi, nlo = split(jnp.transpose(jnp.broadcast_to(norm, (E, E))))
                wide = jnp.concatenate([jnp.concatenate([hi, nhi], axis=1),
                                        jnp.concatenate([lo, nlo], axis=1)], axis=0)
                f = fq[h, rows(b), :]
                both = dot(jnp.concatenate([f, f], axis=1), wide)
                inv = 1.0 / (den[h, rows(b), :] + both[:, E:])
                out = (att[h, rows(b), :] + both[:, :E]) * inv
                den[h, rows(b), :] = inv
                att[h, rows(b), :] = out
                sq = sq + out * out
                pr = pr + cv[h, rows(b), :].astype(F32) * gain_ref[pl.ds(h, 1), :] * out
                full[i] = full[i] + kvb[h, b]
            acc[0, rows(b), :] = sq
            acc[1, rows(b), :] = pr

    def share(d):
        return pltpu.make_async_remote_copy(
            src_ref=stat, dst_ref=stat_in.at[d - 1],
            send_sem=ss.at[d - 1], recv_sem=rs.at[d - 1],
            device_id=zpeer(d), device_id_type=MESH)

    def norms():
        for b in range(nblk):
            for i in range(2):
                stat[i:i + 1, b * block:(b + 1) * block] = jnp.sum(
                    jnp.transpose(acc[i, rows(b), :]), axis=0, keepdims=True)
        for d in range(1, n_head):
            share(d).start()
        for d in range(1, n_head):
            share(d).wait_recv()
        total = stat[...]
        for d in range(1, n_head):
            total = total + stat_in[d - 1]
        scale = lax.rsqrt(total[0:1] / width + 1e-06)
        pull = scale * scale * scale * total[1:2] / width
        for b in range(nblk):
            for i, x in enumerate((scale, pull)):
                x = x[:, b * block:(b + 1) * block]
                acc[i, rows(b), :] = jnp.transpose(jnp.broadcast_to(x, (E, block)))

    def gradient(h):
        gain = gain_ref[pl.ds(h, 1), :]
        total = jnp.zeros((PAY, E), F32)
        for b in range(nblk):
            scale, pull = acc[0, rows(b), :], acc[1, rows(b), :]
            out, inv = att[h, rows(b), :], den[h, rows(b), :]
            sg = scale * gain
            om[h, rows(b), :] = (out * sg).astype(BF16)
            d = sg * cv[h, rows(b), :].astype(F32) - out * pull
            g = (d * inv).astype(BF16)
            gd = -jnp.sum(d * out, axis=1, keepdims=True) * inv
            gn[h, rows(b), :] = g
            den[h, rows(b), :] = gd
            f = fq[h, rows(b), :]
            later = dot(f, g, 0, 0)
            lden = jnp.sum(gd * f.astype(F32), axis=0, keepdims=True)
            part = jnp.concatenate([later, jnp.broadcast_to(lden, (8, E))], axis=0)
            rvb[h, b] = part
            total = total + part
        tot[1, h] = total

    def backward_local(h):
        keep = causal()
        for b in range(nblk):
            f, k, v, g = fq[h, rows(b), :], fk[h, rows(b), :], vv[h, rows(b), :], gn[h, rows(b), :]
            gd = den[h, rows(b), :]
            gw = jnp.concatenate([gd] * (block // E), axis=1)
            m = jnp.where(keep, dot(g, v, 1, 1) + gw, 0.0).astype(BF16)
            far = dot(jnp.concatenate([g, g], axis=1), sh[h, b], 1, 1) + gd * nrm[h, b, 0:1, :]
            dq = dot(m, k) + far
            oq[h, rows(b), :] = (dq * slope(qv[h, rows(b), :])).astype(BF16)
            att[h, rows(b), :] = dot(m, f, 0, 0)
            dvp[h, rows(b), :] = dot(wts[h, b], g, 0, 0)

    def later_sums(h):
        full = pfx[1, h]
        for b in reversed(range(nblk)):
            lat[h, b] = full
            full = full + rvb[h, b]

    def sums(dirn, body, greet=None):
        body(theirs)
        if greet is not None:
            greet()
        swap(dirn, 0).start()

        def step(j):
            body(mine + j)

            @pl.when(j < half - 1)
            def _():
                body(theirs + j + 1)
                swap(dirn, j + 1).start()
            chip_total(dirn, j)
        each(half, step)

    def middle(dirn, local, slot, after=None):
        events = sorted((min(slot(s, j), heads + j), s, j)
                        for s in range(stages) for j in range(half))

        def happen(h):
            for at, s, j in events:
                @pl.when(h == at)
                def _(s=s, j=j):
                    hop_on(dirn, s, j)

        def step(h):
            local(h)
            happen(h)
        each(heads, step)

        def late(j):
            happen(heads + j)
            if after is not None:
                after(j)
        each(half, late)
        if after is None:
            arrive(dirn)

    greeted = len(masks) + n_head - 1
    acc[...] = jnp.zeros_like(acc)
    sums(0, key_sums, lambda: pl.semaphore_wait(barrier, greeted))
    gain_copy.wait()
    middle(0, forward_local, lambda s, j: 1 + 2 * j + 4 * s, forward_state)
    norms()
    sums(1, gradient)
    middle(1, backward_local, lambda s, j: j + 1 + 3 * s)
    each(heads, later_sums)

    drain(0)
    drain(1)
    for d in range(1, n_head):
        share(d).wait_send()


def last(dims, om, oq, kv, vv, fk, att, dvp, lat, mixed_hbm, gq_hbm, gk_hbm, gv_hbm,
         ok, ov, out_sem):
    heads, nblk, block = dims[:3]

    def put(array, h):
        src, dst = ((om, mixed_hbm), (oq, gq_hbm), (ok, gk_hbm), (ov, gv_hbm))[array]
        cols = pl.ds(pl.multiple_of(h * E, E), E)
        return pltpu.make_async_copy(src.at[h], dst.at[:, cols], out_sem.at[array, h])

    def ready(h):
        put(0, h).start()
        put(1, h).start()

    def backward_state(h):
        for b in range(nblk):
            rows = pl.ds(b * block, block)
            full = lat[h, b]
            hi, lo = split(full[:E])
            v, k = vv[h, rows, :], fk[h, rows, :]
            dk = dot(jnp.concatenate([v, v], axis=1), jnp.concatenate([hi, lo], axis=1), 1, 1)
            dk = dk + att[h, rows, :] + full[NORM:NORM + 1]
            ok[h, rows, :] = (dk * slope(kv[h, rows, :])).astype(BF16)
            dv = dot(jnp.concatenate([k, k], axis=1), jnp.concatenate([hi, lo], axis=0))
            ov[h, rows, :] = (dv + dvp[h, rows, :]).astype(BF16)
        put(2, h).start()
        put(3, h).start()

    def finish(h):
        for array in range(4):
            put(array, h).wait()

    each(heads, ready)
    each(heads, backward_state)
    each(heads, finish)


def shards(sizes, queries, keys, values, gain, cotangent):
    n_in, n_out, n_head = sizes
    rows, width = queries.shape
    heads = width // E
    block = min(BLOCK, rows)
    nblk = rows // block
    half = heads // 2
    stages = max((n_in * n_out // 2).bit_length() - 1, 1)
    dims = (heads, nblk, block, n_in, n_out, n_head, width * n_head)
    whole = (heads, rows, E)
    anywhere = pl.BlockSpec(memory_space=pl.ANY)
    dma = pltpu.SemaphoreType.DMA
    half16, full32 = pltpu.VMEM(whole, BF16), pltpu.VMEM(whole, F32)
    held = (half16,) * 5 + (full32,) * 2 + (pltpu.VMEM((heads, nblk, PAY, E), F32),)
    scratch = [
        half16,
        half16,
        half16,
        pltpu.VMEM((heads, nblk, block, block), BF16),
        full32,
        half16,
        pltpu.VMEM((heads, nblk, PAY, E), F32),
        pltpu.VMEM((heads, nblk, PAY, E), F32),
        pltpu.VMEM((heads, nblk, E, 2 * E), BF16),
        pltpu.VMEM((2, heads, PAY, E), F32),
        pltpu.VMEM((2, half, PAY, E), F32),
        pltpu.VMEM((2, stages, half, PAY, E), F32),
        pltpu.VMEM((2, stages, half, PAY, E), F32),
        pltpu.VMEM((2, half, PAY, E), F32),
        pltpu.VMEM((2, heads, PAY, E), F32),
        pltpu.VMEM((2, rows), F32),
        pltpu.VMEM((n_head - 1, 2, rows), F32),
        pltpu.VMEM((2, rows, E), F32),
        pltpu.VMEM((heads, nblk, 8, E), F32),
        pltpu.VMEM((heads, E), F32),
        dma,
        dma((4, heads)),
        dma((2, half)),
        dma((2, half)),
        dma((2, stages, half)),
        dma((2, stages, half)),
        dma((2, half)),
        dma((2, half)),
        dma((n_head - 1,)),
        dma((n_head - 1,)),
    ]
    inside = pl.BlockSpec(memory_space=pltpu.VMEM)
    kept = pl.pallas_call(
        functools.partial(kernel, dims),
        out_shape=held,
        in_specs=[pl.BlockSpec(memory_space=pltpu.MemorySpace.HBM)] * 5,
        out_specs=(inside,) * len(held),
        scratch_shapes=scratch,
        compiler_params=pltpu.CompilerParams(
            collective_id=0, has_side_effects=True, vmem_limit_bytes=VMEM_A
        ),
        cost_estimate=pl.CostEstimate(
            flops=16 * rows * block * width, bytes_accessed=8 * rows * width,
            transcendentals=4 * rows * width,
        ),
    )(queries, keys, values, gain.reshape(heads, E), cotangent)
    out = jax.ShapeDtypeStruct((rows, width), BF16)
    return pl.pallas_call(
        functools.partial(last, dims),
        out_shape=(out,) * 4,
        in_specs=[inside] * len(held),
        out_specs=(anywhere,) * 4,
        scratch_shapes=[half16, half16, dma((4, heads))],
        compiler_params=pltpu.CompilerParams(vmem_limit_bytes=VMEM_B),
        cost_estimate=pl.CostEstimate(
            flops=4 * rows * 2 * E * width, bytes_accessed=8 * rows * width,
            transcendentals=rows * width,
        ),
    )(*kept)


def solution(mesh):
    sizes = tuple(mesh.shape[name] for name in ("seqin", "seqout", "head"))
    rows = P(("seqin", "seqout"), "head")
    return jax.shard_map(
        functools.partial(shards, sizes),
        mesh=mesh,
        in_specs=(rows, rows, rows, P("head"), rows),
        out_specs=(rows,) * 4,
        check_vma=False,
    )
```

```python
import functools

import jax
import jax.numpy as jnp
from jax import lax
from jax.experimental import pallas as pl
from jax.experimental.pallas import tpu as pltpu
from jax.sharding import PartitionSpec as P

E = 128
BLOCK = 256
NORM = E
PAY = E + 8
F32 = jnp.float32
BF16 = jnp.bfloat16
VMEM_A = 48 * 1024 * 1024
VMEM_B = 8 * 1024 * 1024
MESH = pl.DeviceIdType.MESH


def features(x):
    xf = x.astype(F32)
    return jnp.where(xf > 0, xf + 1.0, jnp.exp(jnp.minimum(xf, 0.0))).astype(BF16)


def slope(f):
    return jnp.minimum(f.astype(F32), 1.0)


def dot(a, b, ca=1, cb=0):
    return lax.dot_general(a, b, (((ca,), (cb,)), ((), ())), preferred_element_type=F32)


def split(x):
    hi = x.astype(BF16)
    return hi, (x - hi.astype(F32)).astype(BF16)


def each(n, body):
    def step(j, carry):
        body(j)
        return carry
    lax.fori_loop(0, n, step, 0)


def kernel(dims, q_hbm, k_hbm, v_hbm, g_hbm, c_hbm, om, oq, ok, ov,
           qv, kv, vv, cv, fq, fk, att, dvp, wts, den, gn, kvb, rvb, sh, tot, r0, tx, rx, fin, pfx, stat, stat_in, acc, nrm,
           gain_ref, gain_sem, in_sem, s0, q0, sx, rxs, s2, q2, ss, rs):
    heads, nblk, block, n_in, n_out, n_head, width = dims
    half = heads // 2
    n_seq = n_in * n_out
    nchips = n_seq // 2
    stages = nchips.bit_length() - 1
    a_in, a_out, a_head = lax.axis_index("seqin"), lax.axis_index("seqout"), lax.axis_index("head")
    me = a_in * n_out + a_out
    core = lax.rem(me, 2)
    mine = core * half
    theirs = (1 - core) * half

    def bit(m):
        return lax.rem(lax.div(me, m), 2)

    def peer(m):
        other = me + m - 2 * m * bit(m)
        return (lax.div(other, n_out), lax.rem(other, n_out), a_head)

    def zpeer(d):
        return (a_in, a_out, lax.rem(a_head + d, n_head))

    def fetch(array, h):
        src, dst = ((k_hbm, kv), (v_hbm, vv), (q_hbm, qv), (c_hbm, cv))[array]
        cols = pl.ds(pl.multiple_of(h * E, E), E)
        return pltpu.make_async_copy(src.at[:, cols], dst.at[h], in_sem.at[array, h])

    def start_kv(j):
        for h in (theirs + j, mine + j):
            fetch(0, h).start()
            fetch(1, h).start()

    def start_qc(h):
        fetch(2, h).start()

    each(half, start_kv)
    each(heads, start_qc)
    each(heads, lambda h: fetch(3, h).start())
    gain_copy = pltpu.make_async_copy(g_hbm, gain_ref, gain_sem)
    gain_copy.start()

    barrier = pltpu.get_barrier_semaphore()
    masks = [1 << s for s in range(stages + 1)]
    for m in masks:
        pl.semaphore_signal(barrier, inc=1, device_id=peer(m), device_id_type=MESH)
    for d in range(1, n_head):
        pl.semaphore_signal(barrier, inc=1, device_id=zpeer(d), device_id_type=MESH)

    def swap(dirn, j):
        return pltpu.make_async_remote_copy(
            src_ref=tot.at[dirn, theirs + j], dst_ref=r0.at[dirn, j],
            send_sem=s0.at[dirn, j], recv_sem=q0.at[dirn, j],
            device_id=peer(1), device_id_type=MESH)

    def hop(dirn, s, j):
        return pltpu.make_async_remote_copy(
            src_ref=tx.at[dirn, s, j], dst_ref=rx.at[dirn, s, j],
            send_sem=sx.at[dirn, s, j], recv_sem=rxs.at[dirn, s, j],
            device_id=peer(2 << s), device_id_type=MESH)

    def back(dirn, j):
        return pltpu.make_async_remote_copy(
            src_ref=fin.at[dirn, j], dst_ref=pfx.at[dirn, mine + j],
            send_sem=s2.at[dirn, j], recv_sem=q2.at[dirn, j],
            device_id=peer(1), device_id_type=MESH)

    def back_in(dirn, j):
        return pltpu.make_async_remote_copy(
            src_ref=fin.at[dirn, j], dst_ref=pfx.at[dirn, theirs + j],
            send_sem=s2.at[dirn, j], recv_sem=q2.at[dirn, j],
            device_id=peer(1), device_id_type=MESH)

    def chip_total(dirn, j):
        swap(dirn, j).wait_recv()
        tx[dirn, 0, j] = tot[dirn, mine + j] + r0[dirn, j]
        hop(dirn, 0, j).start()

    def hop_on(dirn, s, j):
        hop(dirn, s, j).wait_recv()
        if s + 1 < stages:
            tx[dirn, s + 1, j] = tx[dirn, s, j] + rx[dirn, s, j]
            hop(dirn, s + 1, j).start()
            return
        total = jnp.zeros((PAY, E), F32)
        for i in range(stages):
            before = bit(2 << i) == 1 - dirn
            total = total + jnp.where(before, rx[dirn, i, j], 0.0)
        near = core == dirn
        own, other = tot[dirn, mine + j], r0[dirn, j]
        fin[dirn, j] = total + jnp.where(near, own, 0.0)
        pfx[dirn, mine + j] = total + jnp.where(near, 0.0, other)
        back(dirn, j).start()

    def drain(dirn):
        def body(j):
            swap(dirn, j).wait_send()
            for s in range(stages):
                hop(dirn, s, j).wait_send()
            back(dirn, j).wait_send()
        each(half, body)

    def rows(b):
        return pl.ds(b * block, block)

    def key_sums(h):
        fetch(0, h).wait()
        fetch(1, h).wait()
        total = jnp.zeros((PAY, E), F32)
        for b in range(nblk):
            f = features(kv[h, rows(b), :])
            fk[h, rows(b), :] = f
            state = dot(f, vv[h, rows(b), :], 0, 0)
            norm = jnp.sum(f.astype(F32), axis=0, keepdims=True)
            part = jnp.concatenate([state, jnp.broadcast_to(norm, (8, E))], axis=0)
            kvb[h, b] = part
            total = total + part
        tot[0, h] = total

    def causal():
        return (lax.broadcasted_iota(jnp.int32, (block, block), 0)
                >= lax.broadcasted_iota(jnp.int32, (block, block), 1))

    def forward_local(h):
        fetch(2, h).wait()
        keep = causal()
        ones = jnp.ones((block, E), BF16)
        for b in range(nblk):
            f = features(qv[h, rows(b), :])
            fq[h, rows(b), :] = f
            w = jnp.where(keep, dot(f, fk[h, rows(b), :], 1, 1), 0.0).astype(BF16)
            wts[h, b] = w
            both = dot(w, jnp.concatenate([vv[h, rows(b), :], ones], axis=1))
            att[h, rows(b), :] = both[:, :E]
            den[h, rows(b), :] = both[:, E:]

    def forward_state(j):
        back_in(0, j).wait_recv()
        pair = (mine + j, theirs + j)
        full = []
        for h in pair:
            fetch(3, h).wait()
            full.append(pfx[0, h])
        for b in range(nblk):
            sq, pr = acc[0, rows(b), :], acc[1, rows(b), :]
            for i, h in enumerate(pair):
                hi, lo = split(full[i][:E])
                sh[h, b] = jnp.concatenate([hi, lo], axis=1)
                norm = full[i][NORM:NORM + 1]
                nrm[h, b] = jnp.broadcast_to(norm, (8, E))
                nhi, nlo = split(jnp.transpose(jnp.broadcast_to(norm, (E, E))))
                wide = jnp.concatenate([jnp.concatenate([hi, nhi], axis=1),
                                        jnp.concatenate([lo, nlo], axis=1)], axis=0)
                f = fq[h, rows(b), :]
                both = dot(jnp.concatenate([f, f], axis=1), wide)
                inv = 1.0 / (den[h, rows(b), :] + both[:, E:])
                out = (att[h, rows(b), :] + both[:, :E]) * inv
                den[h, rows(b), :] = inv
                att[h, rows(b), :] = out
                sq = sq + out * out
                pr = pr + cv[h, rows(b), :].astype(F32) * gain_ref[pl.ds(h, 1), :] * out
                full[i] = full[i] + kvb[h, b]
            acc[0, rows(b), :] = sq
            acc[1, rows(b), :] = pr

    def share(d):
        return pltpu.make_async_remote_copy(
            src_ref=stat, dst_ref=stat_in.at[d - 1],
            send_sem=ss.at[d - 1], recv_sem=rs.at[d - 1],
            device_id=zpeer(d), device_id_type=MESH)

    def norms():
        for b in range(nblk):
            for i in range(2):
                stat[i:i + 1, b * block:(b + 1) * block] = jnp.sum(
                    jnp.transpose(acc[i, rows(b), :]), axis=0, keepdims=True)
        for d in range(1, n_head):
            share(d).start()
        for d in range(1, n_head):
            share(d).wait_recv()
        total = stat[...]
        for d in range(1, n_head):
            total = total + stat_in[d - 1]
        scale = lax.rsqrt(total[0:1] / width + 1e-06)
        pull = scale * scale * scale * total[1:2] / width
        for b in range(nblk):
            for i, x in enumerate((scale, pull)):
                x = x[:, b * block:(b + 1) * block]
                acc[i, rows(b), :] = jnp.transpose(jnp.broadcast_to(x, (E, block)))

    def gradient(h):
        gain = gain_ref[pl.ds(h, 1), :]
        total = jnp.zeros((PAY, E), F32)
        for b in range(nblk):
            scale, pull = acc[0, rows(b), :], acc[1, rows(b), :]
            out, inv = att[h, rows(b), :], den[h, rows(b), :]
            sg = scale * gain
            om[h, rows(b), :] = (out * sg).astype(BF16)
            d = sg * cv[h, rows(b), :].astype(F32) - out * pull
            g = (d * inv).astype(BF16)
            gd = -jnp.sum(d * out, axis=1, keepdims=True) * inv
            gn[h, rows(b), :] = g
            den[h, rows(b), :] = gd
            f = fq[h, rows(b), :]
            later = dot(f, g, 0, 0)
            lden = jnp.sum(gd * f.astype(F32), axis=0, keepdims=True)
            part = jnp.concatenate([later, jnp.broadcast_to(lden, (8, E))], axis=0)
            rvb[h, b] = part
            total = total + part
        tot[1, h] = total

    def backward_local(h):
        keep = causal()
        for b in range(nblk):
            f, k, v, g = fq[h, rows(b), :], fk[h, rows(b), :], vv[h, rows(b), :], gn[h, rows(b), :]
            gd = den[h, rows(b), :]
            gw = jnp.concatenate([gd] * (block // E), axis=1)
            m = jnp.where(keep, dot(g, v, 1, 1) + gw, 0.0).astype(BF16)
            far = dot(jnp.concatenate([g, g], axis=1), sh[h, b], 1, 1) + gd * nrm[h, b, 0:1, :]
            dq = dot(m, k) + far
            oq[h, rows(b), :] = (dq * slope(f)).astype(BF16)
            att[h, rows(b), :] = dot(m, f, 0, 0)
            dvp[h, rows(b), :] = dot(wts[h, b], g, 0, 0)

    def backward_state(j):
        back_in(1, j).wait_recv()
        for h in (mine + j, theirs + j):
            full = pfx[1, h]
            for b in reversed(range(nblk)):
                hi, lo = split(full[:E])
                v, k = vv[h, rows(b), :], fk[h, rows(b), :]
                dk = dot(jnp.concatenate([v, v], axis=1), jnp.concatenate([hi, lo], axis=1), 1, 1)
                dk = dk + att[h, rows(b), :] + full[NORM:NORM + 1]
                ok[h, rows(b), :] = (dk * slope(k)).astype(BF16)
                dv = dot(jnp.concatenate([k, k], axis=1), jnp.concatenate([hi, lo], axis=0))
                ov[h, rows(b), :] = (dv + dvp[h, rows(b), :]).astype(BF16)
                full = full + rvb[h, b]

    def sums(dirn, body, greet=None):
        body(theirs)
        if greet is not None:
            greet()
        swap(dirn, 0).start()

        def step(j):
            body(mine + j)

            @pl.when(j < half - 1)
            def _():
                body(theirs + j + 1)
                swap(dirn, j + 1).start()
            chip_total(dirn, j)
        each(half, step)

    def middle(dirn, local, slot, after):
        events = sorted((min(slot(s, j), heads + j), s, j)
                        for s in range(stages) for j in range(half))

        def happen(h):
            for at, s, j in events:
                @pl.when(h == at)
                def _(s=s, j=j):
                    hop_on(dirn, s, j)

        def step(h):
            local(h)
            happen(h)
        each(heads, step)

        def late(j):
            happen(heads + j)
            after(j)
        each(half, late)

    greeted = len(masks) + n_head - 1
    acc[...] = jnp.zeros_like(acc)
    sums(0, key_sums, lambda: pl.semaphore_wait(barrier, greeted))
    gain_copy.wait()
    middle(0, forward_local, lambda s, j: 1 + 2 * j + 4 * s, forward_state)
    norms()
    sums(1, gradient)
    middle(1, backward_local, lambda s, j: j + 1 + 3 * s, backward_state)

    drain(0)
    drain(1)
    for d in range(1, n_head):
        share(d).wait_send()


def last(heads, om, oq, ok, ov, mixed_hbm, gq_hbm, gk_hbm, gv_hbm, out_sem):
    def put(array, h):
        src, dst = ((om, mixed_hbm), (oq, gq_hbm), (ok, gk_hbm), (ov, gv_hbm))[array]
        cols = pl.ds(pl.multiple_of(h * E, E), E)
        return pltpu.make_async_copy(src.at[h], dst.at[:, cols], out_sem.at[array, h])

    def begin(h):
        for array in range(4):
            put(array, h).start()

    def finish(h):
        for array in range(4):
            put(array, h).wait()

    each(heads, begin)
    each(heads, finish)


def shards(sizes, queries, keys, values, gain, cotangent):
    n_in, n_out, n_head = sizes
    rows, width = queries.shape
    heads = width // E
    block = min(BLOCK, rows)
    nblk = rows // block
    half = heads // 2
    stages = max((n_in * n_out // 2).bit_length() - 1, 1)
    dims = (heads, nblk, block, n_in, n_out, n_head, width * n_head)
    whole = (heads, rows, E)
    anywhere = pl.BlockSpec(memory_space=pl.ANY)
    dma = pltpu.SemaphoreType.DMA
    half16, full32 = pltpu.VMEM(whole, BF16), pltpu.VMEM(whole, F32)
    held = (half16,) * 4
    scratch = [half16] * 6 + [
        full32,
        full32,
        pltpu.VMEM((heads, nblk, block, block), BF16),
        full32,
        half16,
        pltpu.VMEM((heads, nblk, PAY, E), F32),
        pltpu.VMEM((heads, nblk, PAY, E), F32),
        pltpu.VMEM((heads, nblk, E, 2 * E), BF16),
        pltpu.VMEM((2, heads, PAY, E), F32),
        pltpu.VMEM((2, half, PAY, E), F32),
        pltpu.VMEM((2, stages, half, PAY, E), F32),
        pltpu.VMEM((2, stages, half, PAY, E), F32),
        pltpu.VMEM((2, half, PAY, E), F32),
        pltpu.VMEM((2, heads, PAY, E), F32),
        pltpu.VMEM((2, rows), F32),
        pltpu.VMEM((n_head - 1, 2, rows), F32),
        pltpu.VMEM((2, rows, E), F32),
        pltpu.VMEM((heads, nblk, 8, E), F32),
        pltpu.VMEM((heads, E), F32),
        dma,
        dma((4, heads)),
        dma((2, half)),
        dma((2, half)),
        dma((2, stages, half)),
        dma((2, stages, half)),
        dma((2, half)),
        dma((2, half)),
        dma((n_head - 1,)),
        dma((n_head - 1,)),
    ]
    inside = pl.BlockSpec(memory_space=pltpu.VMEM)
    kept = pl.pallas_call(
        functools.partial(kernel, dims),
        out_shape=held,
        in_specs=[pl.BlockSpec(memory_space=pltpu.MemorySpace.HBM)] * 5,
        out_specs=(inside,) * len(held),
        scratch_shapes=scratch,
        compiler_params=pltpu.CompilerParams(
            collective_id=0, has_side_effects=True, vmem_limit_bytes=VMEM_A
        ),
        cost_estimate=pl.CostEstimate(
            flops=16 * rows * block * width, bytes_accessed=8 * rows * width,
            transcendentals=4 * rows * width,
        ),
    )(queries, keys, values, gain.reshape(heads, E), cotangent)
    out = jax.ShapeDtypeStruct((rows, width), BF16)
    return pl.pallas_call(
        functools.partial(last, heads),
        out_shape=(out,) * 4,
        in_specs=[inside] * len(held),
        out_specs=(anywhere,) * 4,
        scratch_shapes=[dma((4, heads))],
        compiler_params=pltpu.CompilerParams(vmem_limit_bytes=VMEM_B),
        cost_estimate=pl.CostEstimate(
            flops=0, bytes_accessed=8 * rows * width, transcendentals=0,
        ),
    )(*kept)


def solution(mesh):
    sizes = tuple(mesh.shape[name] for name in ("seqin", "seqout", "head"))
    rows = P(("seqin", "seqout"), "head")
    return jax.shard_map(
        functools.partial(shards, sizes),
        mesh=mesh,
        in_specs=(rows, rows, rows, P("head"), rows),
        out_specs=(rows,) * 4,
        check_vma=False,
    )
```

```python
import functools

import jax
import jax.numpy as jnp
from jax import lax
from jax.experimental import pallas as pl
from jax.experimental.pallas import tpu as pltpu
from jax.sharding import PartitionSpec as P

E = 128
BLOCK = 256
NORM = E
PAY = E + 8
F32 = jnp.float32
BF16 = jnp.bfloat16
VMEM_A = 40 * 1024 * 1024
VMEM_B = 8 * 1024 * 1024
MESH = pl.DeviceIdType.MESH


def features(x):
    xf = x.astype(F32)
    return jnp.where(xf > 0, xf + 1.0, jnp.exp(jnp.minimum(xf, 0.0))).astype(BF16)


def slope(f):
    return jnp.minimum(f.astype(F32), 1.0)


def inverse(x):
    r = pl.reciprocal(x, approx=True)
    return r * (2.0 - x * r)


def dot(a, b, ca=1, cb=0):
    return lax.dot_general(a, b, (((ca,), (cb,)), ((), ())), preferred_element_type=F32)


def split(x):
    hi = x.astype(BF16)
    return hi, (x - hi.astype(F32)).astype(BF16)


def each(n, body):
    def step(j, carry):
        body(j)
        return carry
    lax.fori_loop(0, n, step, 0)


def kernel(dims, q_hbm, k_hbm, v_hbm, g_hbm, c_hbm, om, oq, vv, fk, att, dvp, lat,
           qv, kv, cv, fq, wts, den, gn, kvb, rvb, sh, tot, r0, tx, rx, fin, pfx, stat, stat_in, acc, nrm, mask, gdp,
           gain_ref, gain_sem, in_sem, s0, q0, sx, rxs, s2, q2, ss, rs):
    heads, nblk, block, n_in, n_out, n_head, width = dims
    half = heads // 2
    n_seq = n_in * n_out
    nchips = n_seq // 2
    stages = nchips.bit_length() - 1
    a_in, a_out, a_head = lax.axis_index("seqin"), lax.axis_index("seqout"), lax.axis_index("head")
    me = a_in * n_out + a_out
    core = lax.rem(me, 2)
    mine = core * half
    theirs = (1 - core) * half

    def bit(m):
        return lax.rem(lax.div(me, m), 2)

    def peer(m):
        other = me + m - 2 * m * bit(m)
        return (lax.div(other, n_out), lax.rem(other, n_out), a_head)

    def zpeer(d):
        return (a_in, a_out, lax.rem(a_head + d, n_head))

    def fetch(array, h):
        src, dst = ((k_hbm, kv), (v_hbm, vv), (q_hbm, qv), (c_hbm, cv))[array]
        cols = pl.ds(pl.multiple_of(h * E, E), E)
        return pltpu.make_async_copy(src.at[:, cols], dst.at[h], in_sem.at[array, h])

    def start_kv(j):
        for h in (theirs + j, mine + j):
            fetch(0, h).start()
            fetch(1, h).start()

    def start_qc(h):
        fetch(2, h).start()

    each(half, start_kv)
    each(heads, start_qc)
    each(heads, lambda h: fetch(3, h).start())
    gain_copy = pltpu.make_async_copy(g_hbm, gain_ref, gain_sem)
    gain_copy.start()

    barrier = pltpu.get_barrier_semaphore()
    masks = [1 << s for s in range(stages + 1)]
    for m in masks:
        pl.semaphore_signal(barrier, inc=1, device_id=peer(m), device_id_type=MESH)
    for d in range(1, n_head):
        pl.semaphore_signal(barrier, inc=1, device_id=zpeer(d), device_id_type=MESH)

    def swap(dirn, j):
        return pltpu.make_async_remote_copy(
            src_ref=tot.at[dirn, theirs + j], dst_ref=r0.at[dirn, j],
            send_sem=s0.at[dirn, j], recv_sem=q0.at[dirn, j],
            device_id=peer(1), device_id_type=MESH)

    def hop(dirn, s, j):
        return pltpu.make_async_remote_copy(
            src_ref=tx.at[dirn, s, j], dst_ref=rx.at[dirn, s, j],
            send_sem=sx.at[dirn, s, j], recv_sem=rxs.at[dirn, s, j],
            device_id=peer(2 << s), device_id_type=MESH)

    def back(dirn, j):
        return pltpu.make_async_remote_copy(
            src_ref=fin.at[dirn, j], dst_ref=pfx.at[dirn, mine + j],
            send_sem=s2.at[dirn, j], recv_sem=q2.at[dirn, j],
            device_id=peer(1), device_id_type=MESH)

    def back_in(dirn, j):
        return pltpu.make_async_remote_copy(
            src_ref=fin.at[dirn, j], dst_ref=pfx.at[dirn, theirs + j],
            send_sem=s2.at[dirn, j], recv_sem=q2.at[dirn, j],
            device_id=peer(1), device_id_type=MESH)

    def chip_total(dirn, j):
        swap(dirn, j).wait_recv()
        tx[dirn, 0, j] = tot[dirn, mine + j] + r0[dirn, j]
        hop(dirn, 0, j).start()

    def hop_on(dirn, s, j):
        hop(dirn, s, j).wait_recv()
        if s + 1 < stages:
            tx[dirn, s + 1, j] = tx[dirn, s, j] + rx[dirn, s, j]
            hop(dirn, s + 1, j).start()
            return
        total = jnp.zeros((PAY, E), F32)
        for i in range(stages):
            before = bit(2 << i) == 1 - dirn
            total = total + jnp.where(before, rx[dirn, i, j], 0.0)
        near = core == dirn
        own, other = tot[dirn, mine + j], r0[dirn, j]
        fin[dirn, j] = total + jnp.where(near, own, 0.0)
        pfx[dirn, mine + j] = total + jnp.where(near, 0.0, other)
        back(dirn, j).start()

    def arrive(dirn):
        each(half, lambda j: back_in(dirn, j).wait_recv())

    def drain(dirn):
        def body(j):
            swap(dirn, j).wait_send()
            for s in range(stages):
                hop(dirn, s, j).wait_send()
            back(dirn, j).wait_send()
        each(half, body)

    def rows(b):
        return pl.ds(b * block, block)

    def key_sums(h):
        fetch(0, h).wait()
        fetch(1, h).wait()
        total = jnp.zeros((PAY, E), F32)
        for b in range(nblk):
            f = features(kv[h, rows(b), :])
            fk[h, rows(b), :] = f
            state = dot(f, vv[h, rows(b), :], 0, 0)
            norm = jnp.sum(f.astype(F32), axis=0, keepdims=True)
            part = jnp.concatenate([state, jnp.broadcast_to(norm, (8, E))], axis=0)
            kvb[h, b] = part
            total = total + part
        tot[0, h] = total

    def causal():
        t = lax.broadcasted_iota(jnp.int32, (block, block), 0)
        u = lax.broadcasted_iota(jnp.int32, (block, block), 1)
        mask[0] = jnp.where(t >= u, 1.0, 0.0).astype(BF16)
        mask[1] = jnp.where(t <= u, 1.0, 0.0).astype(BF16)

    def forward_local(h):
        fetch(2, h).wait()
        ones = jnp.ones((block, E), BF16)
        for b in range(nblk):
            f = features(qv[h, rows(b), :])
            fq[h, rows(b), :] = f
            k = fk[h, rows(b), :]
            w = dot(f, k, 1, 1).astype(BF16) * mask[0]
            wts[h, b] = dot(k, f, 1, 1).astype(BF16) * mask[1]
            both = dot(w, jnp.concatenate([vv[h, rows(b), :], ones], axis=1))
            att[h, rows(b), :] = both[:, :E]
            den[h, rows(b), :] = both[:, E:]

    def forward_state(j):
        back_in(0, j).wait_recv()
        pair = (mine + j, theirs + j)
        full = []
        for h in pair:
            fetch(3, h).wait()
            full.append(pfx[0, h])
        for b in range(nblk):
            sq, pr = acc[0, rows(b), :], acc[1, rows(b), :]
            for i, h in enumerate(pair):
                hi, lo = split(full[i][:E])
                sh[h, b] = jnp.concatenate([hi, lo], axis=1)
                norm = full[i][NORM:NORM + 1]
                nrm[h, b] = jnp.broadcast_to(norm, (8, E))
                nhi, nlo = split(jnp.transpose(jnp.broadcast_to(norm, (E, E))))
                wide = jnp.concatenate([jnp.concatenate([hi, nhi], axis=1),
                                        jnp.concatenate([lo, nlo], axis=1)], axis=0)
                f = fq[h, rows(b), :]
                both = dot(jnp.concatenate([f, f], axis=1), wide)
                inv = inverse(den[h, rows(b), :] + both[:, E:])
                out = (att[h, rows(b), :] + both[:, :E]) * inv
                den[h, rows(b), :] = inv
                att[h, rows(b), :] = out
                sq = sq + out * out
                pr = pr + cv[h, rows(b), :].astype(F32) * gain_ref[pl.ds(h, 1), :] * out
                full[i] = full[i] + kvb[h, b]
            acc[0, rows(b), :] = sq
            acc[1, rows(b), :] = pr

    def share(d):
        return pltpu.make_async_remote_copy(
            src_ref=stat, dst_ref=stat_in.at[d - 1],
            send_sem=ss.at[d - 1], recv_sem=rs.at[d - 1],
            device_id=zpeer(d), device_id_type=MESH)

    def norms():
        for b in range(nblk):
            for i in range(2):
                stat[i:i + 1, b * block:(b + 1) * block] = jnp.sum(
                    jnp.transpose(acc[i, rows(b), :]), axis=0, keepdims=True)
        for d in range(1, n_head):
            share(d).start()
        for d in range(1, n_head):
            share(d).wait_recv()
        total = stat[...]
        for d in range(1, n_head):
            total = total + stat_in[d - 1]
        scale = lax.rsqrt(total[0:1] / width + 1e-06)
        pull = scale * scale * scale * total[1:2] / width
        for b in range(nblk):
            for i, x in enumerate((scale, pull)):
                x = x[:, b * block:(b + 1) * block]
                acc[i, rows(b), :] = jnp.transpose(jnp.broadcast_to(x, (E, block)))

    def gradient(h):
        gain = gain_ref[pl.ds(h, 1), :]
        total = jnp.zeros((PAY, E), F32)
        lane = lax.broadcasted_iota(jnp.int32, (block, E), 1)
        for b in range(nblk):
            scale, pull = acc[0, rows(b), :], acc[1, rows(b), :]
            out, inv = att[h, rows(b), :], den[h, rows(b), :]
            sg = scale * gain
            om[h, rows(b), :] = (out * sg).astype(BF16)
            d = sg * cv[h, rows(b), :].astype(F32) - out * pull
            g = (d * inv).astype(BF16)
            gd = -jnp.sum(d * out, axis=1, keepdims=True) * inv
            gn[h, rows(b), :] = g
            den[h, rows(b), :] = gd
            rest = gd - gd.astype(BF16).astype(F32)
            gdp[h, rows(b), :] = jnp.where(lane == 0, gd, jnp.where(lane == 1, rest, 0.0)).astype(BF16)
            f = fq[h, rows(b), :]
            later = dot(f, g, 0, 0)
            lden = jnp.sum(gd * f.astype(F32), axis=0, keepdims=True)
            part = jnp.concatenate([later, jnp.broadcast_to(lden, (8, E))], axis=0)
            rvb[h, b] = part
            total = total + part
        tot[1, h] = total

    def backward_local(h):
        ones = jnp.ones((block, E), BF16)
        for b in range(nblk):
            f, k, v, g = fq[h, rows(b), :], fk[h, rows(b), :], vv[h, rows(b), :], gn[h, rows(b), :]
            va = jnp.concatenate([v, ones], axis=1)
            ga = jnp.concatenate([g, gdp[h, rows(b), :]], axis=1)
            m = dot(ga, va, 1, 1).astype(BF16) * mask[0]
            mt = dot(va, ga, 1, 1).astype(BF16) * mask[1]
            far = dot(jnp.concatenate([g, g], axis=1), sh[h, b], 1, 1)
            far = far + den[h, rows(b), :] * nrm[h, b, 0:1, :]
            dq = dot(m, k) + far
            oq[h, rows(b), :] = (dq * slope(f)).astype(BF16)
            att[h, rows(b), :] = dot(mt, f)
            dvp[h, rows(b), :] = dot(wts[h, b], g)

    def later_sums(h):
        full = pfx[1, h]
        for b in reversed(range(nblk)):
            lat[h, b] = full
            full = full + rvb[h, b]

    def sums(dirn, body, greet=None):
        body(theirs)
        if greet is not None:
            greet()
        swap(dirn, 0).start()

        def step(j):
            body(mine + j)

            @pl.when(j < half - 1)
            def _():
                body(theirs + j + 1)
                swap(dirn, j + 1).start()
            chip_total(dirn, j)
        each(half, step)

    def middle(dirn, local, slot, after=None):
        events = sorted((min(slot(s, j), heads + j), s, j)
                        for s in range(stages) for j in range(half))

        def happen(h):
            for at, s, j in events:
                @pl.when(h == at)
                def _(s=s, j=j):
                    hop_on(dirn, s, j)

        def step(h):
            local(h)
            happen(h)
        each(heads, step)

        def late(j):
            happen(heads + j)
            if after is not None:
                after(j)
        each(half, late)
        if after is None:
            arrive(dirn)

    greeted = len(masks) + n_head - 1
    acc[...] = jnp.zeros_like(acc)
    causal()
    sums(0, key_sums, lambda: pl.semaphore_wait(barrier, greeted))
    gain_copy.wait()
    middle(0, forward_local, lambda s, j: 1 + 2 * j + 4 * s, forward_state)
    norms()
    sums(1, gradient)
    middle(1, backward_local, lambda s, j: j + 1 + 3 * s)
    each(heads, later_sums)

    drain(0)
    drain(1)
    for d in range(1, n_head):
        share(d).wait_send()


def last(dims, om, oq, vv, fk, att, dvp, lat, mixed_hbm, gq_hbm, gk_hbm, gv_hbm,
         ok, ov, out_sem):
    heads, nblk, block = dims[:3]

    def put(array, h):
        src, dst = ((om, mixed_hbm), (oq, gq_hbm), (ok, gk_hbm), (ov, gv_hbm))[array]
        cols = pl.ds(pl.multiple_of(h * E, E), E)
        return pltpu.make_async_copy(src.at[h], dst.at[:, cols], out_sem.at[array, h])

    def ready(h):
        put(0, h).start()
        put(1, h).start()

    def backward_state(h):
        for b in range(nblk):
            rows = pl.ds(b * block, block)
            full = lat[h, b]
            hi, lo = split(full[:E])
            v, k = vv[h, rows, :], fk[h, rows, :]
            dk = dot(jnp.concatenate([v, v], axis=1), jnp.concatenate([hi, lo], axis=1), 1, 1)
            dk = dk + att[h, rows, :] + full[NORM:NORM + 1]
            ok[h, rows, :] = (dk * slope(k)).astype(BF16)
            dv = dot(jnp.concatenate([k, k], axis=1), jnp.concatenate([hi, lo], axis=0))
            ov[h, rows, :] = (dv + dvp[h, rows, :]).astype(BF16)
        put(2, h).start()
        put(3, h).start()

    def finish(h):
        for array in range(4):
            put(array, h).wait()

    each(heads, ready)
    each(heads, backward_state)
    each(heads, finish)


def shards(sizes, queries, keys, values, gain, cotangent):
    n_in, n_out, n_head = sizes
    rows, width = queries.shape
    heads = width // E
    block = min(BLOCK, rows)
    nblk = rows // block
    half = heads // 2
    stages = max((n_in * n_out // 2).bit_length() - 1, 1)
    dims = (heads, nblk, block, n_in, n_out, n_head, width * n_head)
    whole = (heads, rows, E)
    anywhere = pl.BlockSpec(memory_space=pl.ANY)
    dma = pltpu.SemaphoreType.DMA
    half16, full32 = pltpu.VMEM(whole, BF16), pltpu.VMEM(whole, F32)
    held = (half16,) * 4 + (full32,) * 2 + (pltpu.VMEM((heads, nblk, PAY, E), F32),)
    scratch = [half16] * 4 + [
        pltpu.VMEM((heads, nblk, block, block), BF16),
        full32,
        half16,
        pltpu.VMEM((heads, nblk, PAY, E), F32),
        pltpu.VMEM((heads, nblk, PAY, E), F32),
        pltpu.VMEM((heads, nblk, E, 2 * E), BF16),
        pltpu.VMEM((2, heads, PAY, E), F32),
        pltpu.VMEM((2, half, PAY, E), F32),
        pltpu.VMEM((2, stages, half, PAY, E), F32),
        pltpu.VMEM((2, stages, half, PAY, E), F32),
        pltpu.VMEM((2, half, PAY, E), F32),
        pltpu.VMEM((2, heads, PAY, E), F32),
        pltpu.VMEM((2, rows), F32),
        pltpu.VMEM((n_head - 1, 2, rows), F32),
        pltpu.VMEM((2, rows, E), F32),
        pltpu.VMEM((heads, nblk, 8, E), F32),
        pltpu.VMEM((2, block, block), BF16),
        half16,
        pltpu.VMEM((heads, E), F32),
        dma,
        dma((4, heads)),
        dma((2, half)),
        dma((2, half)),
        dma((2, stages, half)),
        dma((2, stages, half)),
        dma((2, half)),
        dma((2, half)),
        dma((n_head - 1,)),
        dma((n_head - 1,)),
    ]
    inside = pl.BlockSpec(memory_space=pltpu.VMEM)
    kept = pl.pallas_call(
        functools.partial(kernel, dims),
        out_shape=held,
        in_specs=[pl.BlockSpec(memory_space=pltpu.MemorySpace.HBM)] * 5,
        out_specs=(inside,) * len(held),
        scratch_shapes=scratch,
        compiler_params=pltpu.CompilerParams(
            collective_id=0, has_side_effects=True, vmem_limit_bytes=VMEM_A
        ),
        cost_estimate=pl.CostEstimate(
            flops=16 * rows * block * width, bytes_accessed=8 * rows * width,
            transcendentals=4 * rows * width,
        ),
    )(queries, keys, values, gain.reshape(heads, E), cotangent)
    out = jax.ShapeDtypeStruct((rows, width), BF16)
    return pl.pallas_call(
        functools.partial(last, dims),
        out_shape=(out,) * 4,
        in_specs=[inside] * len(held),
        out_specs=(anywhere,) * 4,
        scratch_shapes=[half16, half16, dma((4, heads))],
        compiler_params=pltpu.CompilerParams(vmem_limit_bytes=VMEM_B),
        cost_estimate=pl.CostEstimate(
            flops=4 * rows * 2 * E * width, bytes_accessed=8 * rows * width,
            transcendentals=rows * width,
        ),
    )(*kept)


def solution(mesh):
    sizes = tuple(mesh.shape[name] for name in ("seqin", "seqout", "head"))
    rows = P(("seqin", "seqout"), "head")
    return jax.shard_map(
        functools.partial(shards, sizes),
        mesh=mesh,
        in_specs=(rows, rows, rows, P("head"), rows),
        out_specs=(rows,) * 4,
        check_vma=False,
    )
```

```python
import functools

import jax
import jax.numpy as jnp
from jax import lax
from jax.experimental import pallas as pl
from jax.experimental.pallas import tpu as pltpu
from jax.sharding import PartitionSpec as P

E = 128
BLOCK = 256
NORM = E
PAY = E + 8
F32 = jnp.float32
BF16 = jnp.bfloat16
VMEM_A = 40 * 1024 * 1024
VMEM_B = 8 * 1024 * 1024
MESH = pl.DeviceIdType.MESH


def features(x):
    xf = x.astype(F32)
    return jnp.where(xf > 0, xf + 1.0, jnp.exp(jnp.minimum(xf, 0.0))).astype(BF16)


def slope(f):
    return jnp.minimum(f.astype(F32), 1.0)


def inverse(x):
    r = pl.reciprocal(x, approx=True)
    return r * (2.0 - x * r)


def dot(a, b, ca=1, cb=0):
    return lax.dot_general(a, b, (((ca,), (cb,)), ((), ())), preferred_element_type=F32)


def split(x):
    hi = x.astype(BF16)
    return hi, (x - hi.astype(F32)).astype(BF16)


def each(n, body):
    def step(j, carry):
        body(j)
        return carry
    lax.fori_loop(0, n, step, 0)


def kernel(dims, q_hbm, k_hbm, v_hbm, g_hbm, c_hbm, om, oq, vv, fk, att, dvp, lat,
           qv, kv, cv, fq, wts, den, gn, kvb, rvb, sh, tot, r0, tx, rx, fin, pfx, stat, stat_in, acc, nrm, mask, gdp,
           gain_ref, gain_sem, in_sem, s0, q0, sx, rxs, s2, q2, ss, rs):
    heads, nblk, block, n_in, n_out, n_head, width = dims
    half = heads // 2
    n_seq = n_in * n_out
    nchips = n_seq // 2
    stages = nchips.bit_length() - 1
    a_in, a_out, a_head = lax.axis_index("seqin"), lax.axis_index("seqout"), lax.axis_index("head")
    me = a_in * n_out + a_out
    core = lax.rem(me, 2)
    mine = core * half
    theirs = (1 - core) * half

    def bit(m):
        return lax.rem(lax.div(me, m), 2)

    def peer(m):
        other = me + m - 2 * m * bit(m)
        return (lax.div(other, n_out), lax.rem(other, n_out), a_head)

    cross = stages == 2

    def hop_peer(s):
        a = 2 << s
        b = 2 << (stages - 1 - s) if cross else a
        m = a + core * (b - a)
        at = bit(a) + core * (bit(b) - bit(a))
        other = me + m - 2 * m * at
        return (lax.div(other, n_out), lax.rem(other, n_out), a_head)

    def zpeer(d):
        return (a_in, a_out, lax.rem(a_head + d, n_head))

    def fetch(array, h):
        src, dst = ((k_hbm, kv), (v_hbm, vv), (q_hbm, qv), (c_hbm, cv))[array]
        cols = pl.ds(pl.multiple_of(h * E, E), E)
        return pltpu.make_async_copy(src.at[:, cols], dst.at[h], in_sem.at[array, h])

    def start_kv(j):
        for h in (theirs + j, mine + j):
            fetch(0, h).start()
            fetch(1, h).start()

    def start_qc(h):
        fetch(2, h).start()

    each(half, start_kv)
    each(heads, start_qc)
    each(heads, lambda h: fetch(3, h).start())
    gain_copy = pltpu.make_async_copy(g_hbm, gain_ref, gain_sem)
    gain_copy.start()

    barrier = pltpu.get_barrier_semaphore()
    masks = [1 << s for s in range(stages + 1)]
    for m in masks:
        pl.semaphore_signal(barrier, inc=1, device_id=peer(m), device_id_type=MESH)
    for d in range(1, n_head):
        pl.semaphore_signal(barrier, inc=1, device_id=zpeer(d), device_id_type=MESH)

    def swap(dirn, j):
        return pltpu.make_async_remote_copy(
            src_ref=tot.at[dirn, theirs + j], dst_ref=r0.at[dirn, j],
            send_sem=s0.at[dirn, j], recv_sem=q0.at[dirn, j],
            device_id=peer(1), device_id_type=MESH)

    def hop(dirn, s, j):
        return pltpu.make_async_remote_copy(
            src_ref=tx.at[dirn, s, j], dst_ref=rx.at[dirn, s, j],
            send_sem=sx.at[dirn, s, j], recv_sem=rxs.at[dirn, s, j],
            device_id=hop_peer(s), device_id_type=MESH)

    def back(dirn, j):
        return pltpu.make_async_remote_copy(
            src_ref=fin.at[dirn, j], dst_ref=pfx.at[dirn, mine + j],
            send_sem=s2.at[dirn, j], recv_sem=q2.at[dirn, j],
            device_id=peer(1), device_id_type=MESH)

    def back_in(dirn, j):
        return pltpu.make_async_remote_copy(
            src_ref=fin.at[dirn, j], dst_ref=pfx.at[dirn, theirs + j],
            send_sem=s2.at[dirn, j], recv_sem=q2.at[dirn, j],
            device_id=peer(1), device_id_type=MESH)

    def chip_total(dirn, j):
        swap(dirn, j).wait_recv()
        tx[dirn, 0, j] = tot[dirn, mine + j] + r0[dirn, j]
        hop(dirn, 0, j).start()

    def hop_on(dirn, s, j):
        hop(dirn, s, j).wait_recv()
        if s + 1 < stages:
            own, got = tx[dirn, s, j], rx[dirn, s, j]
            if cross:
                own = jnp.where(jnp.logical_or(core == 0, bit(2) == dirn), own, 0.0)
                got = jnp.where(jnp.logical_or(core == 0, bit(4) == 1 - dirn), got, 0.0)
            tx[dirn, s + 1, j] = own + got
            hop(dirn, s + 1, j).start()
            return
        total = jnp.zeros((PAY, E), F32)
        for i in range(stages):
            before = bit(2 << i) == 1 - dirn
            if cross:
                turned = (bit(4) == 1 - dirn) if i == 0 else (core == 1)
                before = jnp.logical_or(jnp.logical_and(core == 0, before),
                                        jnp.logical_and(core == 1, turned))
            total = total + jnp.where(before, rx[dirn, i, j], 0.0)
        near = core == dirn
        own, other = tot[dirn, mine + j], r0[dirn, j]
        fin[dirn, j] = total + jnp.where(near, own, 0.0)
        pfx[dirn, mine + j] = total + jnp.where(near, 0.0, other)
        back(dirn, j).start()

    def arrive(dirn):
        each(half, lambda j: back_in(dirn, j).wait_recv())

    def drain(dirn):
        def body(j):
            swap(dirn, j).wait_send()
            for s in range(stages):
                hop(dirn, s, j).wait_send()
            back(dirn, j).wait_send()
        each(half, body)

    def rows(b):
        return pl.ds(b * block, block)

    def key_sums(h):
        fetch(0, h).wait()
        fetch(1, h).wait()
        total = jnp.zeros((PAY, E), F32)
        for b in range(nblk):
            f = features(kv[h, rows(b), :])
            fk[h, rows(b), :] = f
            state = dot(f, vv[h, rows(b), :], 0, 0)
            norm = jnp.sum(f.astype(F32), axis=0, keepdims=True)
            part = jnp.concatenate([state, jnp.broadcast_to(norm, (8, E))], axis=0)
            kvb[h, b] = part
            total = total + part
        tot[0, h] = total

    def causal():
        t = lax.broadcasted_iota(jnp.int32, (block, block), 0)
        u = lax.broadcasted_iota(jnp.int32, (block, block), 1)
        mask[0] = jnp.where(t >= u, 1.0, 0.0).astype(BF16)
        mask[1] = jnp.where(t <= u, 1.0, 0.0).astype(BF16)

    def forward_local(h):
        fetch(2, h).wait()
        ones = jnp.ones((block, E), BF16)
        for b in range(nblk):
            f = features(qv[h, rows(b), :])
            fq[h, rows(b), :] = f
            k = fk[h, rows(b), :]
            w = dot(f, k, 1, 1).astype(BF16) * mask[0]
            wts[h, b] = dot(k, f, 1, 1).astype(BF16) * mask[1]
            both = dot(w, jnp.concatenate([vv[h, rows(b), :], ones], axis=1))
            att[h, rows(b), :] = both[:, :E]
            den[h, rows(b), :] = both[:, E:]

    def forward_state(j):
        back_in(0, j).wait_recv()
        pair = (mine + j, theirs + j)
        full = []
        for h in pair:
            fetch(3, h).wait()
            full.append(pfx[0, h])
        for b in range(nblk):
            sq, pr = acc[0, rows(b), :], acc[1, rows(b), :]
            for i, h in enumerate(pair):
                hi, lo = split(full[i][:E])
                sh[h, b] = jnp.concatenate([hi, lo], axis=1)
                norm = full[i][NORM:NORM + 1]
                nrm[h, b] = jnp.broadcast_to(norm, (8, E))
                nhi, nlo = split(jnp.transpose(jnp.broadcast_to(norm, (E, E))))
                wide = jnp.concatenate([jnp.concatenate([hi, nhi], axis=1),
                                        jnp.concatenate([lo, nlo], axis=1)], axis=0)
                f = fq[h, rows(b), :]
                both = dot(jnp.concatenate([f, f], axis=1), wide)
                inv = inverse(den[h, rows(b), :] + both[:, E:])
                out = (att[h, rows(b), :] + both[:, :E]) * inv
                den[h, rows(b), :] = inv
                att[h, rows(b), :] = out
                sq = sq + out * out
                pr = pr + cv[h, rows(b), :].astype(F32) * gain_ref[pl.ds(h, 1), :] * out
                full[i] = full[i] + kvb[h, b]
            acc[0, rows(b), :] = sq
            acc[1, rows(b), :] = pr

    def share(d):
        return pltpu.make_async_remote_copy(
            src_ref=stat, dst_ref=stat_in.at[d - 1],
            send_sem=ss.at[d - 1], recv_sem=rs.at[d - 1],
            device_id=zpeer(d), device_id_type=MESH)

    def norms():
        for b in range(nblk):
            for i in range(2):
                stat[i:i + 1, b * block:(b + 1) * block] = jnp.sum(
                    jnp.transpose(acc[i, rows(b), :]), axis=0, keepdims=True)
        for d in range(1, n_head):
            share(d).start()
        for d in range(1, n_head):
            share(d).wait_recv()
        total = stat[...]
        for d in range(1, n_head):
            total = total + stat_in[d - 1]
        scale = lax.rsqrt(total[0:1] / width + 1e-06)
        pull = scale * scale * scale * total[1:2] / width
        for b in range(nblk):
            for i, x in enumerate((scale, pull)):
                x = x[:, b * block:(b + 1) * block]
                acc[i, rows(b), :] = jnp.transpose(jnp.broadcast_to(x, (E, block)))

    def gradient(h):
        gain = gain_ref[pl.ds(h, 1), :]
        total = jnp.zeros((PAY, E), F32)
        lane = lax.broadcasted_iota(jnp.int32, (block, E), 1)
        for b in range(nblk):
            scale, pull = acc[0, rows(b), :], acc[1, rows(b), :]
            out, inv = att[h, rows(b), :], den[h, rows(b), :]
            sg = scale * gain
            om[h, rows(b), :] = (out * sg).astype(BF16)
            d = sg * cv[h, rows(b), :].astype(F32) - out * pull
            g = (d * inv).astype(BF16)
            gd = -jnp.sum(d * out, axis=1, keepdims=True) * inv
            gn[h, rows(b), :] = g
            den[h, rows(b), :] = gd
            rest = gd - gd.astype(BF16).astype(F32)
            gdp[h, rows(b), :] = jnp.where(lane == 0, gd, jnp.where(lane == 1, rest, 0.0)).astype(BF16)
            f = fq[h, rows(b), :]
            later = dot(f, g, 0, 0)
            lden = jnp.sum(gd * f.astype(F32), axis=0, keepdims=True)
            part = jnp.concatenate([later, jnp.broadcast_to(lden, (8, E))], axis=0)
            rvb[h, b] = part
            total = total + part
        tot[1, h] = total

    def backward_local(h):
        ones = jnp.ones((block, E), BF16)
        for b in range(nblk):
            f, k, v, g = fq[h, rows(b), :], fk[h, rows(b), :], vv[h, rows(b), :], gn[h, rows(b), :]
            va = jnp.concatenate([v, ones], axis=1)
            ga = jnp.concatenate([g, gdp[h, rows(b), :]], axis=1)
            m = dot(ga, va, 1, 1).astype(BF16) * mask[0]
            mt = dot(va, ga, 1, 1).astype(BF16) * mask[1]
            far = dot(jnp.concatenate([g, g], axis=1), sh[h, b], 1, 1)
            far = far + den[h, rows(b), :] * nrm[h, b, 0:1, :]
            dq = dot(m, k) + far
            oq[h, rows(b), :] = (dq * slope(f)).astype(BF16)
            att[h, rows(b), :] = dot(mt, f)
            dvp[h, rows(b), :] = dot(wts[h, b], g)

    def later_sums(h):
        full = pfx[1, h]
        for b in reversed(range(nblk)):
            lat[h, b] = full
            full = full + rvb[h, b]

    def sums(dirn, body, greet=None):
        body(theirs)
        if greet is not None:
            greet()
        swap(dirn, 0).start()

        def step(j):
            body(mine + j)

            @pl.when(j < half - 1)
            def _():
                body(theirs + j + 1)
                swap(dirn, j + 1).start()
            chip_total(dirn, j)
        each(half, step)

    def middle(dirn, local, slot, after=None):
        events = sorted((min(slot(s, j), heads + j - 1), s, j)
                        for s in range(stages) for j in range(half))

        def happen(h):
            for at, s, j in events:
                @pl.when(h == at)
                def _(s=s, j=j):
                    hop_on(dirn, s, j)

        def step(h):
            local(h)
            happen(h)
        each(heads, step)

        def late(j):
            if after is not None:
                after(j)
            happen(heads + j)
        each(half, late)
        if after is None:
            arrive(dirn)

    greeted = len(masks) + n_head - 1
    acc[...] = jnp.zeros_like(acc)
    causal()
    sums(0, key_sums, lambda: pl.semaphore_wait(barrier, greeted))
    gain_copy.wait()
    middle(0, forward_local, lambda s, j: 1 + 2 * j + 4 * s, forward_state)
    norms()
    sums(1, gradient)
    middle(1, backward_local, lambda s, j: j + 3 * s)
    each(heads, later_sums)

    drain(0)
    drain(1)
    for d in range(1, n_head):
        share(d).wait_send()


def last(dims, om, oq, vv, fk, att, dvp, lat, mixed_hbm, gq_hbm, gk_hbm, gv_hbm,
         ok, ov, out_sem):
    heads, nblk, block = dims[:3]

    def put(array, h):
        src, dst = ((om, mixed_hbm), (oq, gq_hbm), (ok, gk_hbm), (ov, gv_hbm))[array]
        cols = pl.ds(pl.multiple_of(h * E, E), E)
        return pltpu.make_async_copy(src.at[h], dst.at[:, cols], out_sem.at[array, h])

    def ready(h):
        put(0, h).start()
        put(1, h).start()

    def backward_state(h):
        for b in range(nblk):
            rows = pl.ds(b * block, block)
            full = lat[h, b]
            hi, lo = split(full[:E])
            v, k = vv[h, rows, :], fk[h, rows, :]
            dk = dot(jnp.concatenate([v, v], axis=1), jnp.concatenate([hi, lo], axis=1), 1, 1)
            dk = dk + att[h, rows, :] + full[NORM:NORM + 1]
            ok[h, rows, :] = (dk * slope(k)).astype(BF16)
            dv = dot(jnp.concatenate([k, k], axis=1), jnp.concatenate([hi, lo], axis=0))
            ov[h, rows, :] = (dv + dvp[h, rows, :]).astype(BF16)
        put(2, h).start()
        put(3, h).start()

    def finish(h):
        for array in range(4):
            put(array, h).wait()

    each(heads, ready)
    each(heads, backward_state)
    each(heads, finish)


def shards(sizes, queries, keys, values, gain, cotangent):
    n_in, n_out, n_head = sizes
    rows, width = queries.shape
    heads = width // E
    block = min(BLOCK, rows)
    nblk = rows // block
    half = heads // 2
    stages = max((n_in * n_out // 2).bit_length() - 1, 1)
    dims = (heads, nblk, block, n_in, n_out, n_head, width * n_head)
    whole = (heads, rows, E)
    anywhere = pl.BlockSpec(memory_space=pl.ANY)
    dma = pltpu.SemaphoreType.DMA
    half16, full32 = pltpu.VMEM(whole, BF16), pltpu.VMEM(whole, F32)
    held = (half16,) * 4 + (full32,) * 2 + (pltpu.VMEM((heads, nblk, PAY, E), F32),)
    scratch = [half16] * 4 + [
        pltpu.VMEM((heads, nblk, block, block), BF16),
        full32,
        half16,
        pltpu.VMEM((heads, nblk, PAY, E), F32),
        pltpu.VMEM((heads, nblk, PAY, E), F32),
        pltpu.VMEM((heads, nblk, E, 2 * E), BF16),
        pltpu.VMEM((2, heads, PAY, E), F32),
        pltpu.VMEM((2, half, PAY, E), F32),
        pltpu.VMEM((2, stages, half, PAY, E), F32),
        pltpu.VMEM((2, stages, half, PAY, E), F32),
        pltpu.VMEM((2, half, PAY, E), F32),
        pltpu.VMEM((2, heads, PAY, E), F32),
        pltpu.VMEM((2, rows), F32),
        pltpu.VMEM((n_head - 1, 2, rows), F32),
        pltpu.VMEM((2, rows, E), F32),
        pltpu.VMEM((heads, nblk, 8, E), F32),
        pltpu.VMEM((2, block, block), BF16),
        half16,
        pltpu.VMEM((heads, E), F32),
        dma,
        dma((4, heads)),
        dma((2, half)),
        dma((2, half)),
        dma((2, stages, half)),
        dma((2, stages, half)),
        dma((2, half)),
        dma((2, half)),
        dma((n_head - 1,)),
        dma((n_head - 1,)),
    ]
    inside = pl.BlockSpec(memory_space=pltpu.VMEM)
    kept = pl.pallas_call(
        functools.partial(kernel, dims),
        out_shape=held,
        in_specs=[pl.BlockSpec(memory_space=pltpu.MemorySpace.HBM)] * 5,
        out_specs=(inside,) * len(held),
        scratch_shapes=scratch,
        compiler_params=pltpu.CompilerParams(
            collective_id=0, has_side_effects=True, vmem_limit_bytes=VMEM_A
        ),
        cost_estimate=pl.CostEstimate(
            flops=16 * rows * block * width, bytes_accessed=8 * rows * width,
            transcendentals=4 * rows * width,
        ),
    )(queries, keys, values, gain.reshape(heads, E), cotangent)
    out = jax.ShapeDtypeStruct((rows, width), BF16)
    return pl.pallas_call(
        functools.partial(last, dims),
        out_shape=(out,) * 4,
        in_specs=[inside] * len(held),
        out_specs=(anywhere,) * 4,
        scratch_shapes=[half16, half16, dma((4, heads))],
        compiler_params=pltpu.CompilerParams(vmem_limit_bytes=VMEM_B),
        cost_estimate=pl.CostEstimate(
            flops=4 * rows * 2 * E * width, bytes_accessed=8 * rows * width,
            transcendentals=rows * width,
        ),
    )(*kept)


def solution(mesh):
    sizes = tuple(mesh.shape[name] for name in ("seqin", "seqout", "head"))
    rows = P(("seqin", "seqout"), "head")
    return jax.shard_map(
        functools.partial(shards, sizes),
        mesh=mesh,
        in_specs=(rows, rows, rows, P("head"), rows),
        out_specs=(rows,) * 4,
        check_vma=False,
    )
```

```python
import functools

import jax
import jax.numpy as jnp
from jax import lax
from jax.experimental import pallas as pl
from jax.experimental.pallas import tpu as pltpu
from jax.sharding import PartitionSpec as P

E = 128
BLOCK = 256
NORM = E
PAY = E + 8
F32 = jnp.float32
BF16 = jnp.bfloat16
VMEM_A = 40 * 1024 * 1024
VMEM_B = 8 * 1024 * 1024
MESH = pl.DeviceIdType.MESH


def features(x):
    xf = x.astype(F32)
    return jnp.where(xf > 0, xf + 1.0, jnp.exp(jnp.minimum(xf, 0.0))).astype(BF16)


def slope(f):
    return jnp.minimum(f.astype(F32), 1.0)


def inverse(x):
    r = pl.reciprocal(x, approx=True)
    return r * (2.0 - x * r)


def dot(a, b, ca=1, cb=0):
    return lax.dot_general(a, b, (((ca,), (cb,)), ((), ())), preferred_element_type=F32)


def split(x):
    hi = x.astype(BF16)
    return hi, (x - hi.astype(F32)).astype(BF16)


def each(n, body):
    def step(j, carry):
        body(j)
        return carry
    lax.fori_loop(0, n, step, 0)


def kernel(dims, q_hbm, k_hbm, v_hbm, g_hbm, c_hbm, om, oq, vv, fk, att, dvp, lat,
           qv, kv, cv, fq, wts, den, gn, kvb, rvb, sh, tot, r0, tx, rx, fin, pfx, stat, stat_in, acc, nrm, mask, gdp,
           gain_ref, gain_sem, in_sem, s0, q0, sx, rxs, s2, q2, ss, rs):
    heads, nblk, block, n_in, n_out, n_head, width = dims
    half = heads // 2
    n_seq = n_in * n_out
    nchips = n_seq // 2
    stages = nchips.bit_length() - 1
    a_in, a_out, a_head = lax.axis_index("seqin"), lax.axis_index("seqout"), lax.axis_index("head")
    me = a_in * n_out + a_out
    core = lax.rem(me, 2)
    mine = core * half
    theirs = (1 - core) * half

    def bit(m):
        return lax.rem(lax.div(me, m), 2)

    def peer(m):
        other = me + m - 2 * m * bit(m)
        return (lax.div(other, n_out), lax.rem(other, n_out), a_head)

    cross = stages == 2

    def hop_peer(s):
        a = 2 << s
        b = 2 << (stages - 1 - s) if cross else a
        m = a + core * (b - a)
        at = bit(a) + core * (bit(b) - bit(a))
        other = me + m - 2 * m * at
        return (lax.div(other, n_out), lax.rem(other, n_out), a_head)

    def zpeer(d):
        return (a_in, a_out, lax.rem(a_head + d, n_head))

    def fetch(array, h):
        src, dst = ((k_hbm, kv), (v_hbm, vv), (q_hbm, qv), (c_hbm, cv))[array]
        cols = pl.ds(pl.multiple_of(h * E, E), E)
        return pltpu.make_async_copy(src.at[:, cols], dst.at[h], in_sem.at[array, h])

    def start_kv(j):
        for h in (theirs + j, mine + j):
            fetch(0, h).start()
            fetch(1, h).start()

    def start_qc(h):
        fetch(2, h).start()

    each(half, start_kv)
    each(heads, start_qc)
    each(heads, lambda h: fetch(3, h).start())
    gain_copy = pltpu.make_async_copy(g_hbm, gain_ref, gain_sem)
    gain_copy.start()

    barrier = pltpu.get_barrier_semaphore()
    masks = [1 << s for s in range(stages + 1)]
    for m in masks:
        pl.semaphore_signal(barrier, inc=1, device_id=peer(m), device_id_type=MESH)
    for d in range(1, n_head):
        pl.semaphore_signal(barrier, inc=1, device_id=zpeer(d), device_id_type=MESH)

    def swap(dirn, j):
        return pltpu.make_async_remote_copy(
            src_ref=tot.at[dirn, theirs + j], dst_ref=r0.at[dirn, j],
            send_sem=s0.at[dirn, j], recv_sem=q0.at[dirn, j],
            device_id=peer(1), device_id_type=MESH)

    def hop(dirn, s, j):
        return pltpu.make_async_remote_copy(
            src_ref=tx.at[dirn, s, j], dst_ref=rx.at[dirn, s, j],
            send_sem=sx.at[dirn, s, j], recv_sem=rxs.at[dirn, s, j],
            device_id=hop_peer(s), device_id_type=MESH)

    def back(dirn, j):
        return pltpu.make_async_remote_copy(
            src_ref=fin.at[dirn, j], dst_ref=pfx.at[dirn, mine + j],
            send_sem=s2.at[dirn, j], recv_sem=q2.at[dirn, j],
            device_id=peer(1), device_id_type=MESH)

    def back_in(dirn, j):
        return pltpu.make_async_remote_copy(
            src_ref=fin.at[dirn, j], dst_ref=pfx.at[dirn, theirs + j],
            send_sem=s2.at[dirn, j], recv_sem=q2.at[dirn, j],
            device_id=peer(1), device_id_type=MESH)

    def chip_total(dirn, j):
        swap(dirn, j).wait_recv()
        tx[dirn, 0, j] = tot[dirn, mine + j] + r0[dirn, j]
        hop(dirn, 0, j).start()

    def hop_on(dirn, s, j):
        hop(dirn, s, j).wait_recv()
        if s + 1 < stages:
            own, got = tx[dirn, s, j], rx[dirn, s, j]
            if cross:
                own = jnp.where(jnp.logical_or(core == 0, bit(2) == dirn), own, 0.0)
                got = jnp.where(jnp.logical_or(core == 0, bit(4) == 1 - dirn), got, 0.0)
            tx[dirn, s + 1, j] = own + got
            hop(dirn, s + 1, j).start()
            return
        total = jnp.zeros((PAY, E), F32)
        for i in range(stages):
            before = bit(2 << i) == 1 - dirn
            if cross:
                turned = (bit(4) == 1 - dirn) if i == 0 else (core == 1)
                before = jnp.logical_or(jnp.logical_and(core == 0, before),
                                        jnp.logical_and(core == 1, turned))
            total = total + jnp.where(before, rx[dirn, i, j], 0.0)
        near = core == dirn
        own, other = tot[dirn, mine + j], r0[dirn, j]
        fin[dirn, j] = total + jnp.where(near, own, 0.0)
        pfx[dirn, mine + j] = total + jnp.where(near, 0.0, other)
        back(dirn, j).start()

    def arrive(dirn):
        each(half, lambda j: back_in(dirn, j).wait_recv())

    def drain(dirn):
        def body(j):
            swap(dirn, j).wait_send()
            for s in range(stages):
                hop(dirn, s, j).wait_send()
            back(dirn, j).wait_send()
        each(half, body)

    def rows(b):
        return pl.ds(b * block, block)

    def key_sums(h):
        fetch(0, h).wait()
        fetch(1, h).wait()
        total = jnp.zeros((PAY, E), F32)
        for b in range(nblk):
            f = features(kv[h, rows(b), :])
            fk[h, rows(b), :] = f
            state = dot(f, vv[h, rows(b), :], 0, 0)
            norm = jnp.sum(f.astype(F32), axis=0, keepdims=True)
            part = jnp.concatenate([state, jnp.broadcast_to(norm, (8, E))], axis=0)
            kvb[h, b] = part
            total = total + part
        tot[0, h] = total

    def causal():
        t = lax.broadcasted_iota(jnp.int32, (block, block), 0)
        u = lax.broadcasted_iota(jnp.int32, (block, block), 1)
        mask[0] = jnp.where(t >= u, 1.0, 0.0).astype(BF16)
        mask[1] = jnp.where(t <= u, 1.0, 0.0).astype(BF16)

    def forward_local(h):
        fetch(2, h).wait()
        ones = jnp.ones((block, E), BF16)
        for b in range(nblk):
            f = features(qv[h, rows(b), :])
            fq[h, rows(b), :] = f
            k = fk[h, rows(b), :]
            w = dot(f, k, 1, 1).astype(BF16) * mask[0]
            wts[h, b] = dot(k, f, 1, 1).astype(BF16) * mask[1]
            both = dot(w, jnp.concatenate([vv[h, rows(b), :], ones], axis=1))
            att[h, rows(b), :] = both[:, :E]
            den[h, rows(b), :] = both[:, E:]

    def forward_state(j):
        back_in(0, j).wait_recv()
        pair = (mine + j, theirs + j)
        full = []
        for h in pair:
            fetch(3, h).wait()
            full.append(pfx[0, h])
        for b in range(nblk):
            sq, pr = acc[0, rows(b), :], acc[1, rows(b), :]
            for i, h in enumerate(pair):
                hi, lo = split(full[i][:E])
                sh[h, b] = jnp.concatenate([hi, lo], axis=1)
                norm = full[i][NORM:NORM + 1]
                nrm[h, b] = jnp.broadcast_to(norm, (8, E))
                nhi, nlo = split(jnp.transpose(jnp.broadcast_to(norm, (E, E))))
                wide = jnp.concatenate([jnp.concatenate([hi, nhi], axis=1),
                                        jnp.concatenate([lo, nlo], axis=1)], axis=0)
                f = fq[h, rows(b), :]
                both = dot(jnp.concatenate([f, f], axis=1), wide)
                inv = inverse(den[h, rows(b), :] + both[:, E:])
                out = (att[h, rows(b), :] + both[:, :E]) * inv
                den[h, rows(b), :] = inv
                att[h, rows(b), :] = out
                sq = sq + out * out
                pr = pr + cv[h, rows(b), :].astype(F32) * gain_ref[pl.ds(h, 1), :] * out
                full[i] = full[i] + kvb[h, b]
            acc[0, rows(b), :] = sq
            acc[1, rows(b), :] = pr

    def share(d):
        return pltpu.make_async_remote_copy(
            src_ref=stat, dst_ref=stat_in.at[d - 1],
            send_sem=ss.at[d - 1], recv_sem=rs.at[d - 1],
            device_id=zpeer(d), device_id_type=MESH)

    def norms():
        for b in range(nblk):
            for i in range(2):
                stat[i:i + 1, b * block:(b + 1) * block] = jnp.sum(
                    jnp.transpose(acc[i, rows(b), :]), axis=0, keepdims=True)
        for d in range(1, n_head):
            share(d).start()
        for d in range(1, n_head):
            share(d).wait_recv()
        total = stat[...]
        for d in range(1, n_head):
            total = total + stat_in[d - 1]
        scale = lax.rsqrt(total[0:1] / width + 1e-06)
        pull = scale * scale * scale * total[1:2] / width
        for b in range(nblk):
            for i, x in enumerate((scale, pull)):
                x = x[:, b * block:(b + 1) * block]
                acc[i, rows(b), :] = jnp.transpose(jnp.broadcast_to(x, (E, block)))

    def gradient(h):
        gain = gain_ref[pl.ds(h, 1), :]
        total = jnp.zeros((PAY, E), F32)
        lane = lax.broadcasted_iota(jnp.int32, (block, E), 1)
        for b in range(nblk):
            scale, pull = acc[0, rows(b), :], acc[1, rows(b), :]
            out, inv = att[h, rows(b), :], den[h, rows(b), :]
            sg = scale * gain
            om[h, rows(b), :] = (out * sg).astype(BF16)
            d = sg * cv[h, rows(b), :].astype(F32) - out * pull
            g = (d * inv).astype(BF16)
            gd = -jnp.sum(d * out, axis=1, keepdims=True) * inv
            gn[h, rows(b), :] = g
            den[h, rows(b), :] = gd
            rest = gd - gd.astype(BF16).astype(F32)
            gdp[h, rows(b), :] = jnp.where(lane == 0, gd, jnp.where(lane == 1, rest, 0.0)).astype(BF16)
            f = fq[h, rows(b), :]
            later = dot(f, g, 0, 0)
            lden = jnp.sum(gd * f.astype(F32), axis=0, keepdims=True)
            part = jnp.concatenate([later, jnp.broadcast_to(lden, (8, E))], axis=0)
            rvb[h, b] = part
            total = total + part
        tot[1, h] = total

    def backward_local(h):
        ones = jnp.ones((block, E), BF16)
        for b in range(nblk):
            f, k, v, g = fq[h, rows(b), :], fk[h, rows(b), :], vv[h, rows(b), :], gn[h, rows(b), :]
            va = jnp.concatenate([v, ones], axis=1)
            ga = jnp.concatenate([g, gdp[h, rows(b), :]], axis=1)
            m = dot(ga, va, 1, 1).astype(BF16) * mask[0]
            mt = dot(va, ga, 1, 1).astype(BF16) * mask[1]
            far = dot(jnp.concatenate([g, g], axis=1), sh[h, b], 1, 1)
            far = far + den[h, rows(b), :] * nrm[h, b, 0:1, :]
            dq = dot(m, k) + far
            oq[h, rows(b), :] = (dq * slope(f)).astype(BF16)
            att[h, rows(b), :] = dot(mt, f)
            dvp[h, rows(b), :] = dot(wts[h, b], g)

    def later_sums(h):
        full = pfx[1, h]
        for b in reversed(range(nblk)):
            lat[h, b] = full
            full = full + rvb[h, b]

    def sums(dirn, body, greet=None):
        body(theirs)
        if greet is not None:
            greet()
        swap(dirn, 0).start()

        def step(j):
            body(mine + j)

            @pl.when(j < half - 1)
            def _():
                body(theirs + j + 1)
                swap(dirn, j + 1).start()
            chip_total(dirn, j)
        each(half, step)

    def middle(dirn, local, slot, after=None):
        events = sorted((min(slot(s, j), heads + j - 1), s, j)
                        for s in range(stages) for j in range(half))

        def happen(h):
            for at, s, j in events:
                @pl.when(h == at)
                def _(s=s, j=j):
                    hop_on(dirn, s, j)

        def step(h):
            local(h)
            happen(h)
        each(heads, step)

        def late(j):
            if after is not None:
                after(j)
            happen(heads + j)
        each(half, late)
        if after is None:
            arrive(dirn)

    greeted = len(masks) + n_head - 1
    acc[...] = jnp.zeros_like(acc)
    causal()
    sums(0, key_sums, lambda: pl.semaphore_wait(barrier, greeted))
    gain_copy.wait()
    middle(0, forward_local, lambda s, j: 1 + j + 4 * s, forward_state)
    norms()
    sums(1, gradient)
    middle(1, backward_local, lambda s, j: j + 3 * s)
    each(heads, later_sums)

    drain(0)
    drain(1)
    for d in range(1, n_head):
        share(d).wait_send()


def last(dims, om, oq, vv, fk, att, dvp, lat, mixed_hbm, gq_hbm, gk_hbm, gv_hbm,
         ok, ov, out_sem):
    heads, nblk, block = dims[:3]

    def put(array, h):
        src, dst = ((om, mixed_hbm), (oq, gq_hbm), (ok, gk_hbm), (ov, gv_hbm))[array]
        cols = pl.ds(pl.multiple_of(h * E, E), E)
        return pltpu.make_async_copy(src.at[h], dst.at[:, cols], out_sem.at[array, h])

    def ready(h):
        put(0, h).start()
        put(1, h).start()

    def backward_state(h):
        for b in range(nblk):
            rows = pl.ds(b * block, block)
            full = lat[h, b]
            hi, lo = split(full[:E])
            v, k = vv[h, rows, :], fk[h, rows, :]
            dk = dot(jnp.concatenate([v, v], axis=1), jnp.concatenate([hi, lo], axis=1), 1, 1)
            dk = dk + att[h, rows, :] + full[NORM:NORM + 1]
            ok[h, rows, :] = (dk * slope(k)).astype(BF16)
            dv = dot(jnp.concatenate([k, k], axis=1), jnp.concatenate([hi, lo], axis=0))
            ov[h, rows, :] = (dv + dvp[h, rows, :]).astype(BF16)
        put(2, h).start()
        put(3, h).start()

    def finish(h):
        for array in range(4):
            put(array, h).wait()

    each(heads, ready)
    each(heads, backward_state)
    each(heads, finish)


def shards(sizes, queries, keys, values, gain, cotangent):
    n_in, n_out, n_head = sizes
    rows, width = queries.shape
    heads = width // E
    block = min(BLOCK, rows)
    nblk = rows // block
    half = heads // 2
    stages = max((n_in * n_out // 2).bit_length() - 1, 1)
    dims = (heads, nblk, block, n_in, n_out, n_head, width * n_head)
    whole = (heads, rows, E)
    anywhere = pl.BlockSpec(memory_space=pl.ANY)
    dma = pltpu.SemaphoreType.DMA
    half16, full32 = pltpu.VMEM(whole, BF16), pltpu.VMEM(whole, F32)
    held = (half16,) * 4 + (full32,) * 2 + (pltpu.VMEM((heads, nblk, PAY, E), F32),)
    scratch = [half16] * 4 + [
        pltpu.VMEM((heads, nblk, block, block), BF16),
        full32,
        half16,
        pltpu.VMEM((heads, nblk, PAY, E), F32),
        pltpu.VMEM((heads, nblk, PAY, E), F32),
        pltpu.VMEM((heads, nblk, E, 2 * E), BF16),
        pltpu.VMEM((2, heads, PAY, E), F32),
        pltpu.VMEM((2, half, PAY, E), F32),
        pltpu.VMEM((2, stages, half, PAY, E), F32),
        pltpu.VMEM((2, stages, half, PAY, E), F32),
        pltpu.VMEM((2, half, PAY, E), F32),
        pltpu.VMEM((2, heads, PAY, E), F32),
        pltpu.VMEM((2, rows), F32),
        pltpu.VMEM((n_head - 1, 2, rows), F32),
        pltpu.VMEM((2, rows, E), F32),
        pltpu.VMEM((heads, nblk, 8, E), F32),
        pltpu.VMEM((2, block, block), BF16),
        half16,
        pltpu.VMEM((heads, E), F32),
        dma,
        dma((4, heads)),
        dma((2, half)),
        dma((2, half)),
        dma((2, stages, half)),
        dma((2, stages, half)),
        dma((2, half)),
        dma((2, half)),
        dma((n_head - 1,)),
        dma((n_head - 1,)),
    ]
    inside = pl.BlockSpec(memory_space=pltpu.VMEM)
    kept = pl.pallas_call(
        functools.partial(kernel, dims),
        out_shape=held,
        in_specs=[pl.BlockSpec(memory_space=pltpu.MemorySpace.HBM)] * 5,
        out_specs=(inside,) * len(held),
        scratch_shapes=scratch,
        compiler_params=pltpu.CompilerParams(
            collective_id=0, has_side_effects=True, vmem_limit_bytes=VMEM_A
        ),
        cost_estimate=pl.CostEstimate(
            flops=16 * rows * block * width, bytes_accessed=8 * rows * width,
            transcendentals=4 * rows * width,
        ),
    )(queries, keys, values, gain.reshape(heads, E), cotangent)
    out = jax.ShapeDtypeStruct((rows, width), BF16)
    return pl.pallas_call(
        functools.partial(last, dims),
        out_shape=(out,) * 4,
        in_specs=[inside] * len(held),
        out_specs=(anywhere,) * 4,
        scratch_shapes=[half16, half16, dma((4, heads))],
        compiler_params=pltpu.CompilerParams(vmem_limit_bytes=VMEM_B),
        cost_estimate=pl.CostEstimate(
            flops=4 * rows * 2 * E * width, bytes_accessed=8 * rows * width,
            transcendentals=rows * width,
        ),
    )(*kept)


def solution(mesh):
    sizes = tuple(mesh.shape[name] for name in ("seqin", "seqout", "head"))
    rows = P(("seqin", "seqout"), "head")
    return jax.shard_map(
        functools.partial(shards, sizes),
        mesh=mesh,
        in_specs=(rows, rows, rows, P("head"), rows),
        out_specs=(rows,) * 4,
        check_vma=False,
    )
```
